256 devices in a mesh: dp: 8 (over y, x_hi), ctx: 32 (over z, x_lo, core).
Axes of the slice: x: 4 (x_hi: 2, x_lo: 2; x = x_hi * 2 + x_lo), y: 4, z: 8, core: 2. Of those that a mesh axis runs over, the one named last changes fastest.
Arguments:
- span_ids: int32 [8, 64], P('dp'), may hold values from 0 to 63, as said below
- q_nope: bfloat16 [8, 4096, 1024], P('dp', 'ctx'), may hold values from -4 to 4
- q_rope: bfloat16 [8, 4096, 512], P('dp', 'ctx'), may hold values from -4 to 4
- w_uk: bfloat16 [8, 128, 512], replicated, may hold values from -1 to 1
- latent: bfloat16 [8, 4096, 512], P('dp', 'ctx'), may hold values from -4 to 4
- rope_key: bfloat16 [8, 4096, 64], P('dp', 'ctx'), may hold values from -4 to 4
- w_uv: bfloat16 [8, 512, 128], replicated, may hold values from -0.25 to 0.25
- d_out: bfloat16 [8, 4096, 1024], P('dp', 'ctx'), may hold values from -6 to 6
- lse: float32 [8, 4096, 8], P('dp', 'ctx'), as said below
- saved_out: bfloat16 [8, 4096, 4096], P('dp', 'ctx'), may hold values from -4 to 4, as said below
Outputs:
- d_q_nope: bfloat16 [8, 4096, 1024], P('dp', 'ctx')
- d_q_rope: bfloat16 [8, 4096, 512], P('dp', 'ctx')
- d_latent: bfloat16 [8, 4096, 512], P('dp', 'ctx')
- d_rope_key: bfloat16 [8, 4096, 64], P('dp', 'ctx')
- d_w_uk: float32 [8, 128, 512], replicated
- d_w_uv: float32 [8, 512, 128], replicated
The draws below stay inside these ranges and needn't reach their ends.
Inputs may be any that keep to these rules, and one draw needn't show every extreme that they name: `span_ids`: the stored spans 2 i and 2 i + 1 of a sequence are its spans c and 2 * 32 - 1 - c for some c; every span is stored once. `lse`: the log-sum-exp over allowed keys of the scores of the forward pass. `saved_out`: the forward pass's softmax-weighted sum of allowed latent rows.
All inputs are finite; a program needn't handle non-finite values.
Results may differ from the reference program's by a relative error of at most 0.025.
Values may be sent and summed in bfloat16 or wider, within the bound.
No kernel may reach another device: no remote copies, remote signals or barrier semaphores. Data moves between devices by JAX's collectives and lax.ppermute only.
A program may use at most 128 MiB of HBM per device.

```python
import jax
import jax.numpy as jnp
from jax import lax

H = 8
HD = 128
DC = 512
DR = 64
CH = 64
SEQ = 4096
SEQS = 8
N_CTX = 32


def span_table(key):
    base_key = jax.random.fold_in(key, 11)

    def one_sequence(sub_key):
        order = jax.random.permutation(sub_key, N_CTX).astype(jnp.int32)
        return jnp.stack([order, 2 * N_CTX - 1 - order], axis=1).reshape(2 * N_CTX)
    return jax.vmap(one_sequence)(jax.random.split(base_key, SEQS))


def rough_values(key, shape):
    first_key = jax.random.fold_in(key, 0)
    normal_part = jnp.clip(jax.random.normal(first_key, shape, jnp.float32), -4.0, 4.0)
    values = normal_part
    return values


def float_inputs(key):
    nope_all = rough_values(jax.random.fold_in(key, 21), (SEQS, SEQ, H * HD))
    rope_all = rough_values(jax.random.fold_in(key, 22), (SEQS, SEQ, H * DR))
    key_weight = rough_values(jax.random.fold_in(key, 23), (H, HD, DC)) * HD ** (-0.5)
    latent_all = rough_values(jax.random.fold_in(key, 24), (SEQS, SEQ, DC))
    rotary_all = rough_values(jax.random.fold_in(key, 25), (SEQS, SEQ, DR))
    return (nope_all.astype(jnp.bfloat16), rope_all.astype(jnp.bfloat16), key_weight.astype(jnp.bfloat16), latent_all.astype(jnp.bfloat16), rotary_all.astype(jnp.bfloat16))


def forward_stats(key):
    span_all = span_table(key)
    nope_all, rope_all, key_weight, latent_all, rotary_all = float_inputs(key)
    scaling = (HD + DR) ** (-0.5)

    def one_sequence(items):
        span_row, nope_seq, rope_seq, latent_seq, rotary_seq = items
        token_idx = jnp.arange(SEQ, dtype=jnp.int32)
        places = span_row[token_idx // CH] * CH + token_idx % CH
        allowed = places[None, :] <= places[:, None]

        def one_head(head_items):
            nope_part, rope_part, w_head = head_items
            q_latent = jnp.dot(nope_part, w_head, preferred_element_type=jnp.float32).astype(jnp.bfloat16)
            scores = (jnp.dot(q_latent, latent_seq.T, preferred_element_type=jnp.float32) + jnp.dot(rope_part, rotary_seq.T, preferred_element_type=jnp.float32)) * scaling
            scores = jnp.where(allowed, scores, -1e+30)
            top_score = jnp.max(scores, axis=1, keepdims=True)
            expo = jnp.exp(scores - top_score)
            totals = jnp.sum(expo, axis=1, keepdims=True)
            lse_row = top_score[:, 0] + jnp.log(totals[:, 0])
            output = jnp.dot(expo / totals, latent_seq.astype(jnp.float32), precision=lax.Precision.HIGHEST)
            return (lse_row, output.astype(jnp.bfloat16))
        per_head = (nope_seq.reshape(SEQ, H, HD).transpose(1, 0, 2), rope_seq.reshape(SEQ, H, DR).transpose(1, 0, 2), key_weight)
        lse_rows, outputs = lax.map(one_head, per_head)
        return (lse_rows.T, outputs.transpose(1, 0, 2).reshape(SEQ, H * DC))
    return lax.map(one_sequence, (span_all, nope_all, rope_all, latent_all, rotary_all))


def draw_span_ids(key, part):
    shared = span_table(key)
    return shared


def draw_q_nope(key, part):
    shared = float_inputs(key)
    return shared[0]


def draw_q_rope(key, part):
    shared = float_inputs(key)
    return shared[1]


def draw_w_uk(key, part):
    shared = float_inputs(key)
    return shared[2]


def draw_latent(key, part):
    shared = float_inputs(key)
    return shared[3]


def draw_rope_key(key, part):
    shared = float_inputs(key)
    return shared[4]


def draw_lse(key, part):
    shared = forward_stats(key)
    return shared[0]


def draw_saved_out(key, part):
    shared = forward_stats(key)
    return shared[1]


def levels(key, dims, cuts, least, high):
    loudness = 1.0
    for dim, blocks in cuts:
        steps = jax.random.uniform(jax.random.fold_in(jax.random.fold_in(key, 6), dim), (blocks,), jnp.float32, least / len(cuts), high / len(cuts))
        loudness = loudness * jnp.repeat(jnp.exp(steps), dims[dim] // blocks).reshape((-1,) + (1,) * (len(dims) - 1 - dim))
    return loudness


def centred(own_key, extent, scale, limit, cuts=(), held_as=jnp.bfloat16):
    entries = jax.random.normal(own_key, extent, jnp.float32) * scale
    if len(cuts) > 0:
        entries = levels(own_key, extent, cuts, -0.22, 0.18) * entries
    return jnp.clip(entries, min=-limit, max=limit).astype(held_as)


def setup_inputs(seed: int = 0) -> dict:
    keys = jax.random.split(jax.random.key(seed), 11)
    span_ids = draw_span_ids(jax.random.fold_in(keys[10], 71), 0)
    q_nope = draw_q_nope(jax.random.fold_in(keys[10], 71), 0)
    q_rope = draw_q_rope(jax.random.fold_in(keys[10], 71), 0)
    w_uk = draw_w_uk(jax.random.fold_in(keys[10], 71), 0)
    latent = draw_latent(jax.random.fold_in(keys[10], 71), 0)
    rope_key = draw_rope_key(jax.random.fold_in(keys[10], 71), 0)
    w_uv = centred(keys[6], (H, DC, HD), DC ** -0.5, 0.25)
    d_out = centred(keys[7], (SEQS, SEQ, H * HD), 1.0, 6.0, ((0, 8), (1, 32)))
    lse = draw_lse(jax.random.fold_in(keys[10], 71), 0)
    saved_out = draw_saved_out(jax.random.fold_in(keys[10], 71), 0)
    return {"span_ids": span_ids, "q_nope": q_nope, "q_rope": q_rope, "w_uk": w_uk, "latent": latent, "rope_key": rope_key, "w_uv": w_uv, "d_out": d_out, "lse": lse, "saved_out": saved_out}


def sequence_grads(span_row, nope_seq, rope_seq, latent_seq, key_seq, grad_seq, lse_seq, saved_seq, w_uk, w_uv):
    token_idx = jnp.arange(SEQ, dtype=jnp.int32)
    places = span_row[token_idx // CH] * CH + token_idx % CH
    allowed = places[None, :] <= places[:, None]
    scaling = (HD + DR) ** -0.5
    per_head = (
        nope_seq.reshape(SEQ, H, HD).transpose(1, 0, 2),
        rope_seq.reshape(SEQ, H, DR).transpose(1, 0, 2),
        grad_seq.reshape(SEQ, H, HD).transpose(1, 0, 2),
        lse_seq.T,
        saved_seq.reshape(SEQ, H, DC).transpose(1, 0, 2),
        w_uk,
        w_uv,
    )

    def head_step(running, items):
        lat_total, rope_total = running
        nope_part, rope_part, grad_part, lse_part, saved_part, w_key, w_value = items
        q_latent = jnp.dot(nope_part, w_key, preferred_element_type=jnp.float32).astype(jnp.bfloat16)
        scores = (jnp.dot(q_latent, latent_seq.T, preferred_element_type=jnp.float32)
                  + jnp.dot(rope_part, key_seq.T, preferred_element_type=jnp.float32)) * scaling
        probs = jnp.exp(jnp.where(allowed, scores - lse_part[:, None], -1e30))
        grad_latent = jnp.dot(grad_part, w_value.T, preferred_element_type=jnp.float32).astype(jnp.bfloat16)
        deltas = jnp.sum(grad_latent.astype(jnp.float32) * saved_part.astype(jnp.float32), axis=1)
        dprobs = jnp.dot(grad_latent, latent_seq.T, preferred_element_type=jnp.float32)
        dscores = (probs * (dprobs - deltas[:, None]) * scaling).astype(jnp.bfloat16)
        probs_b = probs.astype(jnp.bfloat16)
        dq_latent = jnp.dot(dscores, latent_seq, preferred_element_type=jnp.float32).astype(jnp.bfloat16)
        dq_rope = jnp.dot(dscores, key_seq, preferred_element_type=jnp.float32).astype(jnp.bfloat16)
        dq_nope = jnp.dot(dq_latent, w_key.T, preferred_element_type=jnp.float32).astype(jnp.bfloat16)
        key_grad = jnp.dot(nope_part.T, dq_latent, preferred_element_type=jnp.float32)
        value_grad = jnp.dot(saved_part.T, grad_part, preferred_element_type=jnp.float32)
        lat_total = (lat_total + jnp.dot(probs_b.T, grad_latent, preferred_element_type=jnp.float32)
                     + jnp.dot(dscores.T, q_latent, preferred_element_type=jnp.float32))
        rope_total = rope_total + jnp.dot(dscores.T, rope_part, preferred_element_type=jnp.float32)
        return (lat_total, rope_total), (dq_nope, dq_rope, key_grad, value_grad)

    start_state = (jnp.zeros((SEQ, DC), jnp.float32), jnp.zeros((SEQ, DR), jnp.float32))
    (lat_total, rope_total), (dq_nope, dq_rope, key_grad, value_grad) = lax.scan(head_step, start_state, per_head)
    return (dq_nope.transpose(1, 0, 2).reshape(SEQ, H * HD),
            dq_rope.transpose(1, 0, 2).reshape(SEQ, H * DR),
            lat_total.astype(jnp.bfloat16),
            rope_total.astype(jnp.bfloat16),
            key_grad,
            value_grad)


def reference(span_ids, q_nope, q_rope, w_uk, latent, rope_key, w_uv, d_out, lse, saved_out):
    def per_sequence(items):
        span_row, nope_seq, rope_seq, latent_seq, key_seq, grad_seq, lse_seq, saved_seq = items
        return sequence_grads(span_row, nope_seq, rope_seq, latent_seq, key_seq, grad_seq, lse_seq, saved_seq, w_uk, w_uv)

    results = lax.map(per_sequence, (span_ids, q_nope, q_rope, latent, rope_key, d_out, lse, saved_out))
    grad_scale = (SEQS * SEQ) ** -0.5
    key_total = jnp.sum(results[4], axis=0) * grad_scale
    value_total = jnp.sum(results[5], axis=0) * grad_scale
    return results[0], results[1], results[2], results[3], key_total, value_total
```

```python
import functools
import itertools
import math

import jax
import jax.numpy as jnp
from jax import lax
from jax.experimental import pallas as pl
from jax.experimental.pallas import tpu as pltpu
from jax.sharding import PartitionSpec as P

F32 = jnp.float32
BF = jnp.bfloat16
LOG2E = math.log2(math.e)
VMEM_LIMIT = 56 * 1024 * 1024


def dot_nn(a, b):
    return lax.dot_general(a, b, (((1,), (0,)), ((), ())), preferred_element_type=F32)


def dot_nt(a, b):
    return lax.dot_general(a, b, (((1,), (1,)), ((), ())), preferred_element_type=F32)


def dot_tn(a, b):
    return lax.dot_general(a, b, (((0,), (0,)), ((), ())), preferred_element_type=F32)


def own_kernel(heads, do_ref, sv_ref, lse_ref, wv_ref, st_ref, dwv_ref):
    rows = do_ref.shape[0]
    hd = do_ref.shape[1] // heads
    dc = sv_ref.shape[1] // heads
    lane = lax.broadcasted_iota(jnp.int32, (rows, 128), 1)
    acc = jnp.zeros((rows, 128), F32)
    for h in range(heads):
        do = do_ref[:, h * hd : (h + 1) * hd]
        sv = sv_ref[:, h * dc : (h + 1) * dc]
        g = dot_nt(do, wv_ref[h]).astype(BF)
        delta = jnp.sum(g.astype(F32) * sv.astype(F32), axis=1, keepdims=True)
        acc = jnp.where(lane == h, lse_ref[:, h : h + 1] * LOG2E, acc)
        acc = jnp.where(lane == heads + h, delta, acc)
        dwv_ref[h] = dot_tn(sv, do).astype(BF)
    st_ref[...] = acc.T[: 2 * heads]


def own_call(do, sv, lse, wv):
    rows = do.shape[0]
    heads = wv.shape[0]
    return pl.pallas_call(
        functools.partial(own_kernel, heads),
        out_shape=(
            jax.ShapeDtypeStruct((2 * heads, rows), F32),
            jax.ShapeDtypeStruct(wv.shape, BF),
        ),
        compiler_params=pltpu.CompilerParams(vmem_limit_bytes=VMEM_LIMIT),
        name="own_rows",
    )(do, sv, lse, wv)


def attn_kernel(na, nb, heads, spans, scaling, *refs):
    sc = refs[0]
    qn, qr, do, st = (refs[1 + i * na : 1 + (i + 1) * na] for i in range(4))
    at = 1 + 4 * na
    keys = refs[at : at + nb]
    wk, wv = refs[at + nb : at + nb + 2]
    at += nb + 2
    dk = refs[at]
    dqn, dqr = refs[at + 1], refs[at + 2]
    dwk = refs[at + 3]
    Q, G, LB, DB, K, KP, DL, DQ = refs[at + 4 :]

    hd, dc = wk.shape[1], wk.shape[2]
    width = K.shape[2]
    dr = dqr.shape[2] // heads
    tokens = dqn.shape[1]
    ch = tokens // 2
    nkb = K.shape[0] // 2
    rows = heads * ch
    per = nb // nkb
    kw = per * ch

    def low_at(c):
        return pl.multiple_of(jnp.where(2 * c < spans, 0, ch), ch)

    def high_at(c):
        return pl.multiple_of(jnp.where(2 * c < spans, ch, 0), ch)

    def low_span(c):
        return jnp.minimum(c, spans - 1 - c)

    lane = lax.broadcasted_iota(jnp.int32, (8, kw), 1)
    kps = [jnp.zeros((8, kw), jnp.int32) for _ in range(2 * nkb)]
    for b in range(nb):
        c = sc[na + b]
        slot = sc[na + nb + b]
        blk = slot // per
        pos = pl.multiple_of((slot % per) * ch, ch)
        K[blk, pl.ds(pos, ch), :] = keys[b][pl.ds(low_at(c), ch), :]
        K[nkb + blk, pl.ds(pos, ch), :] = keys[b][pl.ds(high_at(c), ch), :]
        lo = low_span(c)
        inside = jnp.logical_and(lane >= pos, lane < pos + ch)
        for i in range(nkb):
            here = jnp.logical_and(inside, blk == i)
            kps[i] = jnp.where(here, lo * ch + (lane - pos), kps[i])
            kps[nkb + i] = jnp.where(here, (spans - 1 - lo) * ch + (lane - pos), kps[nkb + i])
    for i in range(2 * nkb):
        KP[i] = kps[i]
    DL[...] = jnp.zeros_like(DL)
    DQ[...] = jnp.zeros_like(DQ)

    for a in range(na):
        c = sc[a]
        stats = jnp.concatenate(
            [st[a][...], jnp.zeros((128 - 2 * heads, tokens), F32)], axis=0
        ).T
        first = 2 * c < spans
        flipped = jnp.concatenate([stats[ch:], stats[:ch]], axis=0)
        stats = jnp.where(first, stats, flipped)
        for h in range(heads):
            ql = dot_nn(qn[a][:, h * hd : (h + 1) * hd], wk[h]).astype(BF)
            gl = dot_nt(do[a][:, h * hd : (h + 1) * hd], wv[h]).astype(BF)
            qrot = qr[a][:, h * dr : (h + 1) * dr]
            to = slice(h * ch, (h + 1) * ch)
            for half in range(2):
                mine = slice(half * ch, (half + 1) * ch)
                other = slice((1 - half) * ch, (2 - half) * ch)
                Q[a, half, to, :dc] = jnp.where(first, ql[mine], ql[other])
                Q[a, half, to, dc : dc + dr] = jnp.where(first, qrot[mine], qrot[other])
                Q[a, half, to, dc + dr :] = jnp.zeros((ch, width - dc - dr), BF)
                G[a, half, to, :] = jnp.where(first, gl[mine], gl[other])
                LB[a, half, to, :] = jnp.broadcast_to(stats[mine, h : h + 1], (ch, 128))
                DB[a, half, to, :] = jnp.broadcast_to(
                    stats[mine, heads + h : heads + h + 1], (ch, 128)
                )

    sub = min(rows, 256)
    wide = kw // 128
    qtok = lax.broadcasted_iota(jnp.int32, (sub, kw), 0) % ch

    def unit(a, half, kb, span):
        kpos = KP[kb][0:1, :]
        for r in range(rows // sub):
            rr = slice(r * sub, (r + 1) * sub)
            q = Q[a, half, rr, :]
            g = G[a, half, rr, :]
            s = dot_nt(q, K[kb])
            dp = dot_nt(g, K[kb, :, :dc])
            lb = jnp.concatenate([LB[a, half, rr, :]] * wide, axis=1)
            db = jnp.concatenate([DB[a, half, rr, :]] * wide, axis=1)
            p = jnp.exp2(s * (scaling * LOG2E) - lb)
            p = jnp.where(kpos <= span * ch + qtok, p, 0.0)
            ds = (p * ((dp - db) * scaling)).astype(BF)
            pb = p.astype(BF)
            DQ[a, half, rr, :] += dot_nn(ds, K[kb])
            DL[kb, :, :dc] += dot_tn(pb, g) + dot_tn(ds, q[:, :dc])
            DL[kb, :, dc:] += dot_tn(ds, q[:, dc:])

    def query_set(a, _):
        c = sc[a]
        lo = low_span(c)
        hi = spans - 1 - lo
        for blk in range(nkb):
            n_low = jnp.int32(0)
            n_high = jnp.int32(0)
            for b in range(nb):
                here = sc[na + nb + b] // per == blk
                lo_b = low_span(sc[na + b])
                n_low += jnp.where(jnp.logical_and(here, lo_b <= lo), 1, 0)
                n_high += jnp.where(jnp.logical_and(here, lo_b >= lo), 1, 0)
            unit(a, 1, blk, hi)

            @pl.when(n_low > 0)
            def _():
                unit(a, 0, blk, lo)

            @pl.when(n_high > 0)
            def _():
                unit(a, 1, nkb + blk, hi)

        return 0

    lax.fori_loop(0, na, query_set, 0)

    for b in range(nb):
        c = sc[na + b]
        slot = sc[na + nb + b]
        blk = slot // per
        pos = pl.multiple_of((slot % per) * ch, ch)
        dk[b, pl.ds(low_at(c), ch), :] = DL[blk, pl.ds(pos, ch), :]
        dk[b, pl.ds(high_at(c), ch), :] = DL[nkb + blk, pl.ds(pos, ch), :]

    for h in range(heads):
        total = jnp.zeros((hd, dc), F32)
        to = slice(h * ch, (h + 1) * ch)
        for a in range(na):
            first = 2 * sc[a] < spans
            d0 = DQ[a, 0, to, :]
            d1 = DQ[a, 1, to, :]
            d = jnp.concatenate(
                [jnp.where(first, d0, d1), jnp.where(first, d1, d0)], axis=0
            ).astype(BF)
            dqn[a, :, h * hd : (h + 1) * hd] = dot_nt(d[:, :dc], wk[h]).astype(BF)
            dqr[a, :, h * dr : (h + 1) * dr] = d[:, dc : dc + dr]
            total += dot_tn(qn[a][:, h * hd : (h + 1) * hd], d[:, :dc])
        dwk[h] = total.astype(BF)


def attn_call(scalars, queries, keys, wk, wv, spans, scaling):
    na, nb = len(queries), len(keys)
    heads, hd, dc = wk.shape
    tokens, width = keys[0].shape
    ch = tokens // 2
    dr = queries[0][1].shape[1] // heads
    per = min(4, nb)
    nkb = nb // per
    rows = heads * ch
    qn, qr, do, st = ([q[i] for q in queries] for i in range(4))
    vmem = pl.BlockSpec(memory_space=pltpu.VMEM)
    n_in = 4 * na + nb + 2
    return pl.pallas_call(
        functools.partial(attn_kernel, na, nb, heads, spans, scaling),
        in_specs=[pl.BlockSpec(memory_space=pltpu.SMEM)] + [vmem] * n_in,
        out_shape=(
            jax.ShapeDtypeStruct((nb, tokens, width), F32),
            jax.ShapeDtypeStruct((na, tokens, heads * hd), BF),
            jax.ShapeDtypeStruct((na, tokens, heads * dr), BF),
            jax.ShapeDtypeStruct((heads, hd, dc), BF),
        ),
        out_specs=(vmem,) * 4,
        scratch_shapes=[
            pltpu.VMEM((na, 2, rows, width), BF),
            pltpu.VMEM((na, 2, rows, dc), BF),
            pltpu.VMEM((na, 2, rows, 128), F32),
            pltpu.VMEM((na, 2, rows, 128), F32),
            pltpu.VMEM((2 * nkb, per * ch, width), BF),
            pltpu.VMEM((2 * nkb, 8, per * ch), jnp.int32),
            pltpu.VMEM((2 * nkb, per * ch, width), F32),
            pltpu.VMEM((na, 2, rows, width), F32),
        ],
        compiler_params=pltpu.CompilerParams(vmem_limit_bytes=VMEM_LIMIT),
        name="attn_grads",
    )(scalars, *qn, *qr, *do, *st, *keys, wk, wv)


def make_local(grid):
    ny, nxh, nz, nxl, nc = grid

    def ctx_perm(x, fn):
        pairs = []
        for z in range(nz):
            for xl in range(nxl):
                for c in range(nc):
                    z2, xl2, c2 = fn(z, xl, c)
                    pairs.append(((z * nxl + xl) * nc + c, (z2 * nxl + xl2) * nc + c2))
        return lax.ppermute(x, "ctx", pairs)

    def dp_perm(x, fn):
        pairs = []
        for y in range(ny):
            for xh in range(nxh):
                y2, xh2 = fn(y, xh)
                pairs.append((y * nxh + xh, y2 * nxh + xh2))
        return lax.ppermute(x, "dp", pairs)

    def z_send(x, s):
        return ctx_perm(x, lambda z, xl, c: ((z + s) % nz, xl, c))

    def x_swap(x):
        return ctx_perm(x, lambda z, xl, c: (z, nxl - 1 - xl, c))

    def c_swap(x):
        return ctx_perm(x, lambda z, xl, c: (z, xl, nc - 1 - c))

    def y_send(x, s):
        return dp_perm(x, lambda y, xh: ((y + s) % ny, xh))

    def all_perm(x, fn):
        pairs = []
        for y, xh, z, xl, c in itertools.product(*map(range, grid)):
            y2, xh2, z2, xl2, c2 = fn(y, xh, z, xl, c)
            src = (((y * nxh + xh) * nz + z) * nxl + xl) * nc + c
            dst = (((y2 * nxh + xh2) * nz + z2) * nxl + xl2) * nc + c2
            pairs.append((src, dst))
        return lax.ppermute(x, ("dp", "ctx"), pairs)

    def x_send(x, s):
        def fn(y, xh, z, xl, c):
            x2 = (xh * nxl + xl + s) % (nxh * nxl)
            return y, x2 // nxl, z, x2 % nxl, c

        return all_perm(x, fn)

    def z_flip(x, bit):
        return ctx_perm(x, lambda z, xl, c: (z ^ bit, xl, c))

    def scatter_sum(x, send, n, me):
        rows = x.shape[0] // n

        def piece(i):
            return lax.dynamic_slice_in_dim(x, (i % n) * rows, rows, 0)

        total = piece(me).astype(F32)
        for s in range(1, n):
            total += send(piece(me + s), s).astype(F32)
        return total.astype(BF)

    def gather(x, send, n, me):
        got = [send(x, s) for s in range(n - 1, 0, -1)] + [x]
        return lax.dynamic_slice_in_dim(
            jnp.concatenate(got + got, axis=0), (n - 1 - me) * x.shape[0], n * x.shape[0], 0
        )

    def all_sum(x, core, xl, xh, y, z):
        def core_send(x, s):
            return c_swap(x)

        along_x = xh * nxl + xl
        x = scatter_sum(x, core_send, nc, core)
        x = scatter_sum(x, y_send, ny, y)
        x = scatter_sum(x, x_send, nxh * nxl, along_x)
        bit = 1
        while bit < nz:
            x = (x.astype(F32) + z_flip(x, bit).astype(F32)).astype(BF)
            bit *= 2
        x = gather(x, x_send, nxh * nxl, along_x)
        x = gather(x, y_send, ny, y)
        return gather(x, core_send, nc, core)

    def local(span_ids, q_nope, q_rope, w_uk, latent, rope_key, w_uv, d_out, lse, saved_out):
        member = lax.axis_index("ctx")
        dp = lax.axis_index("dp")
        core = member % nc
        xl = (member // nc) % nxl
        z = member // (nc * nxl)
        xh = dp % nxh
        y = dp // nxh
        heads, hd, dc = w_uk.shape
        dr = rope_key.shape[2]
        tokens = q_nope.shape[1]
        ch = tokens // 2
        seq_rows = tokens * nz * nxl * nc
        scaling = (hd + dr) ** (-0.5)
        grad_scale = (ny * nxh * seq_rows) ** (-0.5)
        spans = span_ids.shape[1]
        firsts = span_ids[0, ::2]

        def first_of(z_, xl_, c_):
            return firsts[(z_ * nxl + xl_) * nc + c_]

        pad = (-(dc + dr)) % 128
        own_key = jnp.concatenate(
            [latent[0], rope_key[0], jnp.zeros((tokens, pad), BF)], axis=1
        )
        half = nz // 2
        back, ahead = {0: own_key}, {0: own_key}
        for s in range(1, half):
            back[s] = z_send(back[s - 1], 1)
            ahead[s] = z_send(ahead[s - 1], -1)
        far = jnp.concatenate(
            [z_send(back[half - 1][:ch], 1), z_send(ahead[half - 1][ch:], -1)], axis=0
        )
        offsets = [0]
        keys = [own_key]
        for s in range(1, half):
            offsets += [s, -s]
            keys += [ahead[s], back[s]]
        offsets.append(half)
        keys.append(far)

        stats, value_grad = own_call(d_out[0], saved_out[0], lse[0], w_uv)
        q0 = (q_nope[0], q_rope[0], d_out[0], stats)
        q1 = tuple(c_swap(t) for t in q0)
        q2 = tuple(x_swap(t) for t in q0)
        q3 = tuple(c_swap(t) for t in q2)

        qc = jnp.stack(
            [
                first_of(z, xl, core),
                first_of(z, xl, nc - 1 - core),
                first_of(z, nxl - 1 - xl, core),
                first_of(z, nxl - 1 - xl, nc - 1 - core),
            ]
        )
        kc = jnp.stack([first_of((z + o) % nz, xl, core) for o in offsets])
        low = jnp.minimum(kc, spans - 1 - kc)
        slots = jnp.sum((low[None, :] < low[:, None]).astype(jnp.int32), axis=1)
        scalars = jnp.concatenate([qc, kc, slots]).astype(jnp.int32)

        dk, dqn, dqr, dwk = attn_call(
            scalars, [q0, q1, q2, q3], keys, w_uk, w_uv, spans, scaling
        )

        parts = {o: dk[i] for i, o in enumerate(offsets)}
        plus = z_send(parts[half][:ch].astype(BF), 1)
        minus = z_send(parts[half][ch:].astype(BF), -1)
        if half > 1:
            o = half - 1
            up = jnp.concatenate(
                [parts[o][:ch] + plus.astype(F32), parts[o][ch:]], axis=0
            )
            down = jnp.concatenate(
                [parts[-o][:ch], parts[-o][ch:] + minus.astype(F32)], axis=0
            )
            plus, minus = z_send(up.astype(BF), 1), z_send(down.astype(BF), -1)
            for o in range(half - 2, 0, -1):
                up = parts[o] + plus.astype(F32)
                down = parts[-o] + minus.astype(F32)
                plus, minus = z_send(up.astype(BF), 1), z_send(down.astype(BF), -1)
            own = parts[0] + plus.astype(F32) + minus.astype(F32)
        else:
            own = parts[0] + jnp.concatenate([plus, minus], axis=0).astype(F32)
        own = own.astype(BF)
        d_latent = own[None, :, :dc]
        d_rope_key = own[None, :, dc : dc + dr]

        def home(d):
            from_core = c_swap(d[1]), c_swap(d[3])
            mine = d[0].astype(F32) + from_core[0].astype(F32)
            theirs = d[2].astype(F32) + from_core[1].astype(F32)
            return (mine + x_swap(theirs.astype(BF)).astype(F32)).astype(BF)[None]

        d_q_nope = home(dqn)
        d_q_rope = home(dqr)

        dwv = all_sum(value_grad.reshape(-1, hd), core, xl, xh, y, z)
        dwk = all_sum(dwk.reshape(-1, dc), core, xl, xh, y, z)
        d_w_uk = dwk.reshape(heads, hd, dc).astype(F32) * grad_scale
        d_w_uv = dwv.reshape(heads, dc, hd).astype(F32) * grad_scale
        return (d_q_nope, d_q_rope, d_latent, d_rope_key, d_w_uk, d_w_uv)

    return local


def solution(mesh):
    dp, ctx = mesh.shape["dp"], mesh.shape["ctx"]
    grid = (dp // 2, 2, ctx // 4, 2, 2)
    rows = P("dp", "ctx", None)
    in_specs = (P("dp", None), rows, rows, P(), rows, rows, P(), rows, rows, rows)
    out_specs = (rows, rows, rows, rows, P(), P())
    return jax.shard_map(
        make_local(grid), mesh=mesh, in_specs=in_specs, out_specs=out_specs, check_vma=False
    )
```

```python
import functools
import itertools
import math

import jax
import jax.numpy as jnp
from jax import lax
from jax.experimental import pallas as pl
from jax.experimental.pallas import tpu as pltpu
from jax.sharding import PartitionSpec as P

F32 = jnp.float32
BF = jnp.bfloat16
LOG2E = math.log2(math.e)
VMEM = pl.BlockSpec(memory_space=pltpu.VMEM)
SMEM = pl.BlockSpec(memory_space=pltpu.SMEM)
ANY = pl.BlockSpec(memory_space=pl.ANY)


def vmem(mib):
    return pltpu.CompilerParams(vmem_limit_bytes=mib * 1024 * 1024)


def dot_nn(a, b):
    return lax.dot_general(a, b, (((1,), (0,)), ((), ())), preferred_element_type=F32)


def dot_nt(a, b):
    return lax.dot_general(a, b, (((1,), (1,)), ((), ())), preferred_element_type=F32)


def dot_tn(a, b):
    return lax.dot_general(a, b, (((0,), (0,)), ((), ())), preferred_element_type=F32)


def add(*terms):
    return sum(t.astype(F32) for t in terms).astype(BF)


def places(grid, dp, ctx):
    ny, nxh, nz, nxl, nc = grid
    return (
        dp // nxh,
        (dp % nxh) * nxl + (ctx // nc) % nxl,
        ctx // (nc * nxl),
        ctx % nc,
    )


def own_kernel(grid, dp_ref, ctx_ref, qn, qr, do_ref, sv_ref, lse_ref, lat, rope, wv_ref, key, pack, *dwv):
    ny, nxh, nz, nxl, nc = grid
    y, x, z, core = places(grid, dp_ref[0], ctx_ref[0])
    nx = nxh * nxl
    rows = do_ref.shape[0]
    heads, dc, hd = wv_ref.shape
    dr = rope.shape[0]
    group = hd // nx
    key[:, :dc] = lat[...]
    key[:, dc:] = (
        jnp.concatenate([rope[...].astype(F32), jnp.zeros((128 - dr, rows), F32)], axis=0)
        .T.astype(BF)
    )
    per_core = heads // nc
    per_y = per_core // ny
    lane = lax.broadcasted_iota(jnp.int32, (rows, 128), 1)
    part = lane % (2 * heads)
    lse = lse_ref[...] * LOG2E
    gap = jnp.zeros_like(lse)
    rest = jnp.zeros((128 - 6 * heads, rows), F32)
    acc = jnp.concatenate([lse, gap, lse, gap, lse, gap, rest], axis=0).T
    for i, j, k in itertools.product(range(nc), range(ny), range(per_y)):
        h = (core + i) % nc * per_core + (y + j) % ny * per_y + k
        do = do_ref[:, pl.ds(pl.multiple_of(h * hd, hd), hd)]
        sv = sv_ref[:, pl.ds(pl.multiple_of(h * dc, dc), dc)]
        g = dot_nt(do, wv_ref[h]).astype(BF)
        delta = jnp.sum(g.astype(F32) * sv.astype(F32), axis=1, keepdims=True)
        acc = jnp.where(part == heads + h, delta, acc)
        dv = dot_tn(sv, do).astype(BF)
        for n in range(nx):
            at = pl.multiple_of((n - x + nx) % nx * group, group)
            for m in range(dc // hd):
                dwv[i][j * per_y + k, pl.ds(at, group), m * hd : (m + 1) * hd] = dv[
                    m * hd + n * group : m * hd + (n + 1) * group
                ]
    high = acc.astype(BF)
    rest = acc - high.astype(F32)
    mid = rest.astype(BF)
    low = (rest - mid.astype(F32)).astype(BF)
    wn, wr, wd = qn.shape[1], qr.shape[1], do_ref.shape[1]
    pack[:, :wn] = qn[...]
    pack[:, wn : wn + wr] = qr[...]
    pack[:, wn + wr : wn + wr + wd] = do_ref[...]
    pack[:, wn + wr + wd :] = jnp.where(
        lane < 2 * heads, high, jnp.where(lane < 4 * heads, mid, low)
    )


def own_call(grid, dp, ctx, qn, qr, do, sv, lse, lat, rope, wv):
    rows = do.shape[0]
    heads, dc, hd = wv.shape
    nc = grid[4]
    return pl.pallas_call(
        functools.partial(own_kernel, grid),
        in_specs=[SMEM, SMEM] + [VMEM] * 8,
        out_specs=(VMEM,) * (2 + nc),
        out_shape=(
            jax.ShapeDtypeStruct((rows, dc + 128), BF),
            jax.ShapeDtypeStruct((rows, qn.shape[1] + qr.shape[1] + do.shape[1] + 128), BF),
        )
        + (jax.ShapeDtypeStruct((heads // nc, hd, dc), BF),) * nc,
        compiler_params=vmem(60),
        cost_estimate=pl.CostEstimate(flops=4 * 10**9, bytes_accessed=4 * 10**6, transcendentals=0),
        name="own_rows",
    )(dp, ctx, qn, qr, do, sv, lse, lat, rope, wv)


def attn_kernel(grid, offsets, na, heads, spans, scaling, *refs):
    ny, nxh, nz, nxl, nc = grid
    nx = nxh * nxl
    nb = len(offsets)
    ids, dp_ref, ctx_ref = refs[:3]
    packs = refs[3 : 3 + na]
    keys = refs[3 + na : 3 + na + nb]
    wk, wv = refs[3 + na + nb : 5 + na + nb]
    out = refs[5 + na + nb :]
    far, dk, (keep, send), weights = out[:2], out[2 : nb + 1], out[nb + 1 : nb + 3], out[nb + 3 : nb + 3 + nc]
    PK, KC, Q, G, LB, DB, K, KP, DL, DQ, DO, WA, sems = out[nb + 3 + nc :]
    y, x, z, core = places(grid, dp_ref[0], ctx_ref[0])
    xl = x % nxl

    hd, dc = wk.shape[1], wk.shape[2]
    width = K.shape[2]
    tokens = KC.shape[1]
    wn = heads * hd
    wr = DO.shape[2] - wn
    dr = wr // heads
    ch = tokens // 2
    nkb = K.shape[0] // 2
    rows = heads * ch
    per = nb // nkb
    kw = per * ch

    copies = [pltpu.make_async_copy(packs[a], PK.at[a], sems.at[a]) for a in range(na)]
    copies += [pltpu.make_async_copy(keys[b], KC.at[b], sems.at[na + b]) for b in range(nb)]
    for c in copies:
        c.start()

    def first_of(z_, xl_, c_):
        return ids[0, 2 * ((z_ * nxl + xl_) * nc + c_)]

    qc = [
        first_of(z, xl, core),
        first_of(z, nxl - 1 - xl, core),
        first_of(z, xl, nc - 1 - core),
        first_of(z, nxl - 1 - xl, nc - 1 - core),
    ][:na]
    kc = [first_of((z + o + nz) % nz, xl, core) for o in offsets]

    def low_span(c):
        return jnp.minimum(c, spans - 1 - c)

    klow = [low_span(c) for c in kc]
    slots = [sum(jnp.where(other < mine, 1, 0) for other in klow) for mine in klow]

    def pick(values, a):
        out = values[0]
        for i in range(1, len(values)):
            out = jnp.where(a == i, values[i], out)
        return out

    DL[...] = jnp.zeros_like(DL)
    WA[...] = jnp.zeros_like(WA)

    for c in copies[:na]:
        c.wait()

    def prepare(a, _):
        first = 2 * pick(qc, a) < spans
        stats = PK[a, :, wn + wr + heads * hd :].astype(F32)
        stats = stats[:, : 2 * heads] + stats[:, 2 * heads : 4 * heads] + stats[:, 4 * heads : 6 * heads]
        flipped = jnp.concatenate([stats[ch:], stats[:ch]], axis=0)
        stats = jnp.where(first, stats, flipped)
        for h in range(heads):
            ql = dot_nn(PK[a, :, h * hd : (h + 1) * hd], wk[h]).astype(BF)
            gl = dot_nt(PK[a, :, wn + wr + h * hd : wn + wr + (h + 1) * hd], wv[h]).astype(BF)
            qrot = PK[a, :, wn + h * dr : wn + (h + 1) * dr]
            to = slice(h * ch, (h + 1) * ch)
            for half in range(2):
                mine = slice(half * ch, (half + 1) * ch)
                other = slice((1 - half) * ch, (2 - half) * ch)
                Q[a, half, to, :dc] = jnp.where(first, ql[mine], ql[other])
                Q[a, half, to, dc : dc + dr] = jnp.where(first, qrot[mine], qrot[other])
                Q[a, half, to, dc + dr :] = jnp.zeros((ch, width - dc - dr), BF)
                G[a, half, to, :] = jnp.where(first, gl[mine], gl[other])
                LB[a, half, to, :] = jnp.broadcast_to(stats[mine, h : h + 1], (ch, 128))
                DB[a, half, to, :] = jnp.broadcast_to(
                    stats[mine, heads + h : heads + h + 1], (ch, 128)
                )
        return 0

    lax.fori_loop(0, na, prepare, 0)

    for c in copies[na:]:
        c.wait()
    lane = lax.broadcasted_iota(jnp.int32, (8, kw), 1)
    kps = [jnp.zeros((8, kw), jnp.int32) for _ in range(2 * nkb)]
    key_at = []
    for b in range(nb):
        blk = slots[b] // per
        pos = pl.multiple_of((slots[b] % per) * ch, ch)
        first = 2 * kc[b] < spans
        low_at = pl.multiple_of(jnp.where(first, 0, ch), ch)
        high_at = pl.multiple_of(jnp.where(first, ch, 0), ch)
        key_at.append((blk, pos, low_at, high_at))
        K[blk, pl.ds(pos, ch), :] = KC[b, pl.ds(low_at, ch), :]
        K[nkb + blk, pl.ds(pos, ch), :] = KC[b, pl.ds(high_at, ch), :]
        inside = jnp.logical_and(lane >= pos, lane < pos + ch)
        for i in range(nkb):
            here = jnp.logical_and(inside, blk == i)
            kps[i] = jnp.where(here, klow[b] * ch + (lane - pos), kps[i])
            kps[nkb + i] = jnp.where(here, (spans - 1 - klow[b]) * ch + (lane - pos), kps[nkb + i])
    for i in range(2 * nkb):
        KP[i] = kps[i]

    sub = min(rows, 512)
    wide = kw // 128
    qtok = lax.broadcasted_iota(jnp.int32, (sub, kw), 0) % ch

    def unit(a, half, kb, span, fresh):
        kpos = KP[kb][0:1, :]
        dss, pbs = [], []
        for r in range(rows // sub):
            rr = slice(r * sub, (r + 1) * sub)
            s = dot_nt(Q[a, half, rr, :], K[kb])
            dp = dot_nt(G[a, half, rr, :], K[kb, :, :dc])
            lb = jnp.concatenate([LB[a, half, rr, :]] * wide, axis=1)
            db = jnp.concatenate([DB[a, half, rr, :]] * wide, axis=1)
            p = jnp.exp2(s * (scaling * LOG2E) - lb)
            p = jnp.where(kpos <= span * ch + qtok, p, 0.0)
            ds = (p * ((dp - db) * scaling)).astype(BF)
            DQ[half, rr, :] = jnp.where(fresh, 0.0, DQ[half, rr, :]) + dot_nn(ds, K[kb])
            dss.append(ds)
            pbs.append(p.astype(BF))
        ds = jnp.concatenate(dss, axis=0)
        pb = jnp.concatenate(pbs, axis=0)
        DL[kb, :, :dc] += dot_tn(pb, G[a, half]) + dot_tn(ds, Q[a, half, :, :dc])
        DL[kb, :, dc:] += dot_tn(ds, Q[a, half, :, dc:])

    def query_set(a, _):
        c = pick(qc, a)
        lo = low_span(c)
        hi = spans - 1 - lo
        below = sum(jnp.where(k <= lo, 1, 0) for k in klow)
        above = sum(jnp.where(k >= lo, 1, 0) for k in klow)

        @pl.when(below == 0)
        def _():
            DQ[0] = jnp.zeros_like(DQ[0])


        def step(u, _):
            blk = u // 3
            kind = u % 3
            half = jnp.where(kind == 1, 0, 1)
            kb = jnp.where(kind == 2, nkb + blk, blk)
            need = jnp.where(
                kind == 1, below > per * blk, jnp.where(kind == 2, nb - above < per * (blk + 1), True)
            )

            @pl.when(need)
            def _():
                unit(a, half, kb, jnp.where(kind == 1, lo, hi), u < 2)

            return 0

        lax.fori_loop(0, 3 * nkb, step, 0)

        first = 2 * c < spans
        for h in range(heads):
            to = slice(h * ch, (h + 1) * ch)
            d0 = DQ[0, to, dc : dc + dr]
            d1 = DQ[1, to, dc : dc + dr]
            d = jnp.concatenate([jnp.where(first, d0, d1), jnp.where(first, d1, d0)], axis=0)
            DO[a, :, wn + h * dr : wn + (h + 1) * dr] = d.astype(BF)
            d0 = DQ[0, to, :dc]
            d1 = DQ[1, to, :dc]
            d = jnp.concatenate([jnp.where(first, d0, d1), jnp.where(first, d1, d0)], axis=0)
            d = d.astype(BF)
            DO[a, :, h * hd : (h + 1) * hd] = dot_nt(d, wk[h]).astype(BF)
            WA[h] += dot_tn(PK[a, :, h * hd : (h + 1) * hd], d)
        return 0

    lax.fori_loop(0, na, query_set, 0)

    keep[...] = DO[: na // 2]
    send[...] = DO[na // 2 :]
    for b in range(nb):
        blk, pos, low_at, high_at = key_at[b]
        KC[b, pl.ds(low_at, ch), :] = DL[blk, pl.ds(pos, ch), :].astype(BF)
        KC[b, pl.ds(high_at, ch), :] = DL[nkb + blk, pl.ds(pos, ch), :].astype(BF)
        if b < nb - 1:
            dk[b][...] = KC[b]
        else:
            far[0][...] = KC[b, :ch]
            far[1][...] = KC[b, ch:]
    group = hd // nx
    per_core = heads // nc
    per_y = per_core // ny
    for i, j, k in itertools.product(range(nc), range(ny), range(per_y)):
        h = (core + i) % nc * per_core + (y + j) % ny * per_y + k
        for n in range(nx):
            at = pl.multiple_of((n - x + nx) % nx * group, group)
            weights[i][j * per_y + k, pl.ds(at, group), :] = WA[
                h, n * group : (n + 1) * group, :
            ].astype(BF)


def attn_call(grid, offsets, ids, dp, ctx, packs, keys, wk, wv, wr, scaling):
    na, nb = len(packs), len(keys)
    heads, hd, dc = wk.shape
    tokens, width = keys[0].shape
    ch = tokens // 2
    per = min(4, nb)
    nkb = nb // per
    rows = heads * ch
    nc = grid[4]
    out = heads * hd + wr
    return pl.pallas_call(
        functools.partial(attn_kernel, grid, offsets, na, heads, ids.shape[1], scaling),
        in_specs=[SMEM] * 3 + [ANY] * (na + nb) + [VMEM] * 2,
        out_shape=(
            (jax.ShapeDtypeStruct((ch, width), BF),) * 2
            + (jax.ShapeDtypeStruct((tokens, width), BF),) * (nb - 1)
            + (jax.ShapeDtypeStruct((na // 2, tokens, out), BF),) * 2
            + (jax.ShapeDtypeStruct((heads // nc, hd, dc), BF),) * nc
        ),
        out_specs=(VMEM,) * (nb + 3 + nc),
        scratch_shapes=[
            pltpu.VMEM((na,) + packs[0].shape, BF),
            pltpu.VMEM((nb, tokens, width), BF),
            pltpu.VMEM((na, 2, rows, width), BF),
            pltpu.VMEM((na, 2, rows, dc), BF),
            pltpu.VMEM((na, 2, rows, 128), F32),
            pltpu.VMEM((na, 2, rows, 128), F32),
            pltpu.VMEM((2 * nkb, per * ch, width), BF),
            pltpu.VMEM((2 * nkb, 8, per * ch), jnp.int32),
            pltpu.VMEM((2 * nkb, per * ch, width), F32),
            pltpu.VMEM((2, rows, width), F32),
            pltpu.VMEM((na, tokens, out), BF),
            pltpu.VMEM((heads, hd, dc), F32),
            pltpu.SemaphoreType.DMA((na + nb,)),
        ],
        compiler_params=vmem(44),
        cost_estimate=pl.CostEstimate(
            flops=3 * 10**10, bytes_accessed=10**7, transcendentals=10**7
        ),
        name="attn_grads",
    )(ids, dp, ctx, *packs, *keys, wk, wv)


def final_kernel(grid, heads, scale, dp_ref, ctx_ref, key_ref, plus, minus, q_ref, back_ref, *refs):
    ny, nxh, nz, nxl, nc = grid
    nx = nxh * nxl
    pieces, (dqn, dqr, dlat, drope, dwk, dwv) = refs[:-6], refs[-6:]
    dr = drope.shape[0]
    lat = dlat.shape[1]
    if plus.shape[0] == key_ref.shape[0]:
        got = plus[...].astype(F32) + minus[...].astype(F32)
    else:
        got = jnp.concatenate([plus[...].astype(F32), minus[...].astype(F32)], axis=0)
    key = key_ref[...].astype(F32) + got
    dlat[...] = key[:, :lat].astype(BF)
    drope[...] = key[:, lat:].T[:dr].astype(BF)
    q = add(q_ref[0], back_ref[...])
    dqn[...] = q[:, : dqn.shape[1]]
    dqr[...] = q[:, dqn.shape[1] :]
    y, x, z, core = places(grid, dp_ref[0], ctx_ref[0])
    hd = dwk.shape[1]
    dc = dwk.shape[2]
    per_core = heads // nc
    per_y = per_core // ny
    group = hd // nx
    for i, j, n, k in itertools.product(range(nc), range(ny), range(nx), range(per_y)):
        ref = pieces[i * ny + j]
        h = (core + i) % nc * per_core + (y - j + ny) % ny * per_y + k
        at = pl.multiple_of((x - n + nx) % nx * group, group)
        r = (n * 2 * per_y + k) * group
        dwk[h, pl.ds(at, group), :] = ref[r : r + group, :].astype(F32) * scale
        r += per_y * group
        for m in range(dc // hd):
            dwv[h, pl.ds(m * hd + at, group), :] = (
                ref[r : r + group, m * hd : (m + 1) * hd].astype(F32) * scale
            )


def final_call(grid, heads, hd, dr, scale, dp, ctx, key, plus, minus, q, back, pieces):
    tokens = key.shape[0]
    dc = pieces[0].shape[1]
    return pl.pallas_call(
        functools.partial(final_kernel, grid, heads, scale),
        in_specs=[SMEM, SMEM] + [VMEM] * (5 + len(pieces)),
        out_specs=(VMEM,) * 6,
        out_shape=(
            jax.ShapeDtypeStruct((tokens, heads * hd), BF),
            jax.ShapeDtypeStruct((tokens, heads * dr), BF),
            jax.ShapeDtypeStruct((tokens, dc), BF),
            jax.ShapeDtypeStruct((dr, tokens), BF),
            jax.ShapeDtypeStruct((heads, hd, dc), F32),
            jax.ShapeDtypeStruct((heads, dc, hd), F32),
        ),
        compiler_params=vmem(16),
        name="outputs",
    )(dp, ctx, key, plus, minus, q, back, *pieces)


def make_local(grid):
    ny, nxh, nz, nxl, nc = grid
    nx = nxh * nxl

    def all_perm(x, fn):
        pairs = []
        for y, xh, z, xl, c in itertools.product(*map(range, grid)):
            y2, xh2, z2, xl2, c2 = fn(y, xh, z, xl, c)
            src = (((y * nxh + xh) * nz + z) * nxl + xl) * nc + c
            dst = (((y2 * nxh + xh2) * nz + z2) * nxl + xl2) * nc + c2
            pairs.append((src, dst))
        return lax.ppermute(x, ("dp", "ctx"), pairs)

    def z_send(x, s):
        return all_perm(x, lambda y, xh, z, xl, c: (y, xh, (z + s) % nz, xl, c))

    def z_flip(x, bit):
        return all_perm(x, lambda y, xh, z, xl, c: (y, xh, z ^ bit, xl, c))

    def xl_swap(x):
        return all_perm(x, lambda y, xh, z, xl, c: (y, xh, z, nxl - 1 - xl, c))

    def c_swap(x):
        return all_perm(x, lambda y, xh, z, xl, c: (y, xh, z, xl, nc - 1 - c))

    def y_send(x, s):
        return all_perm(x, lambda y, xh, z, xl, c: ((y + s) % ny, xh, z, xl, c))

    def x_send(x, s):
        def fn(y, xh, z, xl, c):
            x2 = (xh * nxl + xl + s) % nx
            return y, x2 // nxl, z, x2 % nxl, c

        return all_perm(x, fn)

    def by_x(x, hd):
        x = x.reshape(ny, x.shape[0] // ny, nx, hd // nx, x.shape[2])
        return x.transpose(0, 2, 1, 3, 4).reshape(ny, nx, -1, x.shape[4])

    def local(span_ids, q_nope, q_rope, w_uk, latent, rope_key, w_uv, d_out, lse, saved_out):
        dp = lax.axis_index("dp").astype(jnp.int32).reshape(1)
        ctx = lax.axis_index("ctx").astype(jnp.int32).reshape(1)
        heads, hd, dc = w_uk.shape
        dr = rope_key.shape[2]
        tokens = q_nope.shape[1]
        ch = tokens // 2
        seq_rows = tokens * nz * nxl * nc
        scaling = (hd + dr) ** (-0.5)
        grad_scale = (ny * nxh * seq_rows) ** (-0.5)

        key, pack, *dwv = own_call(
            grid,
            dp,
            ctx,
            q_nope[0],
            q_rope[0],
            d_out[0],
            saved_out[0],
            lse[0].T,
            latent[0],
            rope_key[0].T,
            w_uv,
        )

        half = nz // 2
        back, ahead = {0: key}, {0: key}
        for s in range(1, half):
            back[s] = z_send(back[s - 1], 1)
            ahead[s] = z_send(ahead[s - 1], -1)
            back[s], ahead[s] = lax.optimization_barrier((back[s], ahead[s]))
        far = jnp.concatenate(
            [z_send(back[half - 1][:ch], 1), z_send(ahead[half - 1][ch:], -1)], axis=0
        )
        offsets = [0]
        keys = [key]
        for s in range(1, half):
            offsets += [s, -s]
            keys += [ahead[s], back[s]]
        offsets.append(half)
        keys.append(far)

        pack_x = xl_swap(pack)
        pack_c = c_swap(pack)
        pack_x, _ = lax.optimization_barrier((pack_x, back[half - 1]))
        packs = [pack, pack_x, pack_c, c_swap(pack_x)]

        dwv, dwv_send = dwv
        dwv_got = c_swap(dwv_send)
        res = attn_call(
            grid, offsets, span_ids, dp, ctx, packs, keys, w_uk, w_uv, heads * dr, scaling
        )
        nb = len(offsets)
        far_up, far_down = res[:2]
        parts = dict(zip(offsets[:-1], res[2 : nb + 1]))
        dq, dq_send, dwk, dwk_send = res[nb + 1 :]

        t = jnp.concatenate(
            [by_x(add(dwk, c_swap(dwk_send)), hd), by_x(add(dwv, dwv_got), hd)], axis=2
        )
        t = add(t[0], *[y_send(t[s], s) for s in range(1, ny)])
        t = add(t[0], *[x_send(t[s], s) for s in range(1, nx)])
        bit = 1
        while bit < nz:
            t = add(t, z_flip(t, bit))
            bit *= 2
        t = jnp.concatenate([t] + [x_send(t, s) for s in range(1, nx)], axis=0)
        pieces = [t] + [y_send(t, s) for s in range(1, ny)]
        pieces += [c_swap(p) for p in pieces]

        plus, minus = z_send(far_up, 1), z_send(far_down, -1)
        for o in range(half - 1, 0, -1):
            if o == half - 1:
                up = jnp.concatenate([add(parts[o][:ch], plus), parts[o][ch:]], axis=0)
                down = jnp.concatenate([parts[-o][:ch], add(parts[-o][ch:], minus)], axis=0)
            else:
                up, down = add(parts[o], plus), add(parts[-o], minus)
            up, down = lax.optimization_barrier((up, down))
            plus, minus = z_send(up, 1), z_send(down, -1)

        q = add(dq, c_swap(dq_send))
        back = xl_swap(q[1])

        d_q_nope, d_q_rope, d_latent, d_rope_key, d_w_uk, d_w_uv = final_call(
            grid, heads, hd, dr, grad_scale, dp, ctx, parts[0], plus, minus, q, back, pieces
        )
        return (d_q_nope[None], d_q_rope[None], d_latent[None], d_rope_key.T[None], d_w_uk, d_w_uv)

    return local


def solution(mesh):
    dp, ctx = mesh.shape["dp"], mesh.shape["ctx"]
    grid = (dp // 2, 2, ctx // 4, 2, 2)
    rows = P("dp", "ctx", None)
    in_specs = (P("dp", None), rows, rows, P(), rows, rows, P(), rows, rows, rows)
    out_specs = (rows, rows, rows, rows, P(), P())
    return jax.shard_map(
        make_local(grid), mesh=mesh, in_specs=in_specs, out_specs=out_specs, check_vma=False
    )
```

```python
import functools
import itertools
import math

import jax
import jax.numpy as jnp
from jax import lax
from jax.experimental import pallas as pl
from jax.experimental.pallas import tpu as pltpu
from jax.sharding import PartitionSpec as P

F32 = jnp.float32
BF = jnp.bfloat16
LOG2E = math.log2(math.e)
VMEM = pl.BlockSpec(memory_space=pltpu.VMEM)
SMEM = pl.BlockSpec(memory_space=pltpu.SMEM)
ANY = pl.BlockSpec(memory_space=pl.ANY)


def vmem(mib):
    return pltpu.CompilerParams(vmem_limit_bytes=mib * 1024 * 1024)


def dot_nn(a, b):
    return lax.dot_general(a, b, (((1,), (0,)), ((), ())), preferred_element_type=F32)


def dot_nt(a, b):
    return lax.dot_general(a, b, (((1,), (1,)), ((), ())), preferred_element_type=F32)


def dot_tn(a, b):
    return lax.dot_general(a, b, (((0,), (0,)), ((), ())), preferred_element_type=F32)


def add(*terms):
    return sum(t.astype(F32) for t in terms).astype(BF)


def places(grid, dp, ctx):
    ny, nxh, nz, nxl, nc = grid
    return (
        dp // nxh,
        (dp % nxh) * nxl + (ctx // nc) % nxl,
        ctx // (nc * nxl),
        ctx % nc,
    )


def own_kernel(grid, dp_ref, ctx_ref, qn, qr, do_ref, sv_ref, lse_ref, wv_ref, pack, *dwv):
    ny, nxh, nz, nxl, nc = grid
    y, x, z, core = places(grid, dp_ref[0], ctx_ref[0])
    nx = nxh * nxl
    rows = do_ref.shape[0]
    heads, dc, hd = wv_ref.shape
    group = hd // nx
    per_core = heads // nc
    per_y = per_core // ny
    lane = lax.broadcasted_iota(jnp.int32, (rows, 128), 1)
    part = lane % (2 * heads)
    lse = lse_ref[...] * LOG2E
    gap = jnp.zeros_like(lse)
    rest = jnp.zeros((128 - 6 * heads, rows), F32)
    acc = jnp.concatenate([lse, gap, lse, gap, lse, gap, rest], axis=0).T
    for i, j, k in itertools.product(range(nc), range(ny), range(per_y)):
        h = (core + i) % nc * per_core + (y + j) % ny * per_y + k
        do = do_ref[:, pl.ds(pl.multiple_of(h * hd, hd), hd)]
        sv = sv_ref[:, pl.ds(pl.multiple_of(h * dc, dc), dc)]
        g = dot_nt(do, wv_ref[h]).astype(BF)
        delta = jnp.sum(g.astype(F32) * sv.astype(F32), axis=1, keepdims=True)
        acc = jnp.where(part == heads + h, delta, acc)
        dv = dot_tn(sv, do).astype(BF)
        for n in range(nx):
            at = pl.multiple_of((n - x + nx) % nx * group, group)
            for m in range(dc // hd):
                dwv[i][j * per_y + k, pl.ds(at, group), m * hd : (m + 1) * hd] = dv[
                    m * hd + n * group : m * hd + (n + 1) * group
                ]
    high = acc.astype(BF)
    rest = acc - high.astype(F32)
    mid = rest.astype(BF)
    low = (rest - mid.astype(F32)).astype(BF)
    wn, wr, wd = qn.shape[1], qr.shape[1], do_ref.shape[1]
    pack[:, :wn] = qn[...]
    pack[:, wn : wn + wr] = qr[...]
    pack[:, wn + wr : wn + wr + wd] = do_ref[...]
    pack[:, wn + wr + wd :] = jnp.where(
        lane < 2 * heads, high, jnp.where(lane < 4 * heads, mid, low)
    )


def own_call(grid, dp, ctx, qn, qr, do, sv, lse, wv):
    rows = do.shape[0]
    heads, dc, hd = wv.shape
    nc = grid[4]
    return pl.pallas_call(
        functools.partial(own_kernel, grid),
        in_specs=[SMEM, SMEM] + [VMEM] * 6,
        out_specs=(VMEM,) * (1 + nc),
        out_shape=(
            jax.ShapeDtypeStruct((rows, qn.shape[1] + qr.shape[1] + do.shape[1] + 128), BF),
        )
        + (jax.ShapeDtypeStruct((heads // nc, hd, dc), BF),) * nc,
        compiler_params=vmem(60),
        cost_estimate=pl.CostEstimate(flops=4 * 10**9, bytes_accessed=4 * 10**6, transcendentals=0),
        name="own_rows",
    )(dp, ctx, qn, qr, do, sv, lse, wv)


def key_kernel(lat, rope, key):
    dc = lat.shape[1]
    pad = jnp.zeros((key.shape[1] - dc - rope.shape[0], rope.shape[1]), F32)
    key[:, :dc] = lat[...]
    key[:, dc:] = jnp.concatenate([rope[...].astype(F32), pad], axis=0).T.astype(BF)


def key_call(lat, rope):
    return pl.pallas_call(
        key_kernel,
        in_specs=[VMEM] * 2,
        out_specs=VMEM,
        out_shape=jax.ShapeDtypeStruct((lat.shape[0], lat.shape[1] + 128), BF),
        compiler_params=vmem(60),
        name="key_rows",
    )(lat, rope)


def attn_kernel(grid, na, heads, spans, scaling, *refs):
    ny, nxh, nz, nxl, nc = grid
    nx = nxh * nxl
    nb = nz
    ids, dp_ref, ctx_ref = refs[:3]
    packs = refs[3 : 3 + na]
    keys = refs[3 + na : 4 + na + nb]
    wk, wv = refs[4 + na + nb : 6 + na + nb]
    out = refs[6 + na + nb :]
    n = 2 + nb // 2
    dk_own, dk_far, dk, dk_send = out[0], out[1], out[2 : n - 1], out[n - 1]
    (keep, send), weights = out[n : n + 2], out[n + 2 : n + 2 + nc]
    PK, KC, Q, G, LB, DB, K, KP, DL, DQ, DO, WA, sems = out[n + 2 + nc :]
    y, x, z, core = places(grid, dp_ref[0], ctx_ref[0])
    offsets = [0] + [o for s in range(1, nb // 2) for o in (-s, s)] + [nb // 2]
    xl = x % nxl

    hd, dc = wk.shape[1], wk.shape[2]
    width = K.shape[2]
    tokens = KC.shape[1]
    wn = heads * hd
    wr = DO.shape[2] - wn
    dr = wr // heads
    ch = tokens // 2
    nkb = K.shape[0] // 2
    rows = heads * ch
    per = nb // nkb
    kw = per * ch

    copies = [pltpu.make_async_copy(
            packs[a], PK.at[pl.ds(a * tokens, tokens)], sems.at[a]
        ) for a in range(na)]
    copies += [
        pltpu.make_async_copy(keys[b].at[pl.ds(0, tokens)], KC.at[b], sems.at[na + b])
        for b in range(nb - 1)
    ]
    own_half = pl.ds(pl.multiple_of(core * ch, ch), ch)
    other_half = pl.ds(pl.multiple_of((1 - core) * ch, ch), ch)
    for b, rows_at in ((nb - 1, pl.ds(0, ch)), (nb, pl.ds(ch, ch))):
        copies.append(
            pltpu.make_async_copy(
                keys[b].at[pl.ds(0, ch)], KC.at[nb - 1, rows_at], sems.at[na + b]
            )
        )
    for c in copies:
        c.start()

    def first_of(z_, xl_, c_):
        return ids[0, 2 * ((z_ * nxl + xl_) * nc + c_)]

    qc = [
        first_of(z, xl, core),
        first_of(z, nxl - 1 - xl, core),
        first_of(z, xl, nc - 1 - core),
        first_of(z, nxl - 1 - xl, nc - 1 - core),
    ][:na]
    kc = [first_of((z + o + nz) % nz, xl, core) for o in offsets]

    def low_span(c):
        return jnp.minimum(c, spans - 1 - c)

    klow = [low_span(c) for c in kc]
    slots = [sum(jnp.where(other < mine, 1, 0) for other in klow) for mine in klow]

    def pick(values, a):
        out = values[0]
        for i in range(1, len(values)):
            out = jnp.where(a == i, values[i], out)
        return out

    DL[...] = jnp.zeros_like(DL)

    for c in copies[:na]:
        c.wait()

    lows = [jnp.where(2 * c < spans, 0, 1) for c in qc]
    stats = PK[:, wn + wr + wn :].astype(F32)
    stats = stats[:, : 2 * heads] + stats[:, 2 * heads : 4 * heads] + stats[:, 4 * heads : 6 * heads]
    for h in range(heads):
        ql = dot_nn(PK[:, h * hd : (h + 1) * hd], wk[h]).astype(BF)
        gl = dot_nt(PK[:, wn + wr + h * hd : wn + wr + (h + 1) * hd], wv[h]).astype(BF)
        qrot = PK[:, wn + h * dr : wn + (h + 1) * dr]
        to = slice(h * ch, (h + 1) * ch)
        for a, slot in itertools.product(range(na), range(2)):
            mine = slice((2 * a + slot) * ch, (2 * a + slot + 1) * ch)
            half = lows[a] if slot == 0 else 1 - lows[a]
            Q[a, half, to, :dc] = ql[mine]
            Q[a, half, to, dc : dc + dr] = qrot[mine]
            Q[a, half, to, dc + dr :] = jnp.zeros((ch, width - dc - dr), BF)
            G[a, half, to, :] = gl[mine]
            LB[a, half, to, :] = jnp.broadcast_to(stats[mine, h : h + 1], (ch, 128))
            DB[a, half, to, :] = jnp.broadcast_to(
                stats[mine, heads + h : heads + h + 1], (ch, 128)
            )

    for c in copies[na:]:
        c.wait()
    lane = lax.broadcasted_iota(jnp.int32, (8, kw), 1)
    kps = [jnp.zeros((8, kw), jnp.int32) for _ in range(2 * nkb)]
    key_at = []
    for b in range(nb):
        blk = slots[b] // per
        pos = pl.multiple_of((slots[b] % per) * ch, ch)
        first = 2 * kc[b] < spans
        low_at = pl.multiple_of(jnp.where(first, 0, ch), ch)
        high_at = pl.multiple_of(jnp.where(first, ch, 0), ch)
        key_at.append((blk, pos, low_at, high_at))
        K[blk, pl.ds(pos, ch), :] = KC[b, pl.ds(low_at, ch), :]
        K[nkb + blk, pl.ds(pos, ch), :] = KC[b, pl.ds(high_at, ch), :]
        inside = jnp.logical_and(lane >= pos, lane < pos + ch)
        for i in range(nkb):
            here = jnp.logical_and(inside, blk == i)
            kps[i] = jnp.where(here, klow[b] * ch + (lane - pos), kps[i])
            kps[nkb + i] = jnp.where(here, (spans - 1 - klow[b]) * ch + (lane - pos), kps[nkb + i])
    for i in range(2 * nkb):
        KP[i] = kps[i]

    sub = min(rows, 256)
    wide = kw // 128
    qtok = lax.broadcasted_iota(jnp.int32, (sub, kw), 0) % ch

    def unit(a, half, kb, span, fresh):
        kpos = KP[kb][0:1, :]

        def scores(r):
            rr = slice(r * sub, (r + 1) * sub)
            return dot_nt(Q[a, half, rr, :], K[kb]), dot_nt(G[a, half, rr, :], K[kb, :, :dc])

        dss, pbs = [], []
        ready = scores(0)
        for r in range(rows // sub):
            rr = slice(r * sub, (r + 1) * sub)
            s, dp = ready
            if r + 1 < rows // sub:
                ready = scores(r + 1)
            lb = jnp.concatenate([LB[a, half, rr, :]] * wide, axis=1)
            db = jnp.concatenate([DB[a, half, rr, :]] * wide, axis=1)
            p = jnp.exp2(s * (scaling * LOG2E) - lb)
            p = jnp.where(kpos <= span * ch + qtok, p, 0.0)
            dss.append((p * ((dp - db) * scaling)).astype(BF))
            pbs.append(p.astype(BF))
        ds = jnp.concatenate(dss, axis=0)
        pb = jnp.concatenate(pbs, axis=0)
        DQ[half] = jnp.where(fresh, 0.0, DQ[half]) + dot_nn(ds, K[kb])
        DL[kb, :, :dc] += dot_tn(pb, G[a, half]) + dot_tn(ds, Q[a, half, :, :dc])
        DL[kb, :, dc:] += dot_tn(ds, Q[a, half, :, dc:])

    def query_set(a, _):
        c = pick(qc, a)
        lo = low_span(c)
        hi = spans - 1 - lo
        below = sum(jnp.where(k <= lo, 1, 0) for k in klow)
        above = sum(jnp.where(k >= lo, 1, 0) for k in klow)

        @pl.when(below == 0)
        def _():
            DQ[0] = jnp.zeros_like(DQ[0])


        def step(u, _):
            blk = u // 3
            kind = u % 3
            half = jnp.where(kind == 1, 0, 1)
            kb = jnp.where(kind == 2, nkb + blk, blk)
            need = jnp.where(
                kind == 1, below > per * blk, jnp.where(kind == 2, nb - above < per * (blk + 1), True)
            )

            @pl.when(need)
            def _():
                unit(a, half, kb, jnp.where(kind == 1, lo, hi), u < 2)

            return 0

        lax.fori_loop(0, 3 * nkb, step, 0)

        low = jnp.where(2 * c < spans, 0, 1)
        for h in range(heads):
            to = slice(h * ch, (h + 1) * ch)
            d = jnp.concatenate([DQ[low, to, :], DQ[1 - low, to, :]], axis=0).astype(BF)
            DO[a, :, wn + h * dr : wn + (h + 1) * dr] = d[:, dc : dc + dr]
            WA[h, pl.ds(pl.multiple_of(a * tokens, tokens), tokens), :] = d[:, :dc]
        return 0

    lax.fori_loop(0, na, query_set, 0)

    for h in range(heads):
        d = dot_nt(WA[h], wk[h]).astype(BF)
        for a in range(na):
            DO[a, :, h * hd : (h + 1) * hd] = d[a * tokens : (a + 1) * tokens]
    keep[...] = DO[: na // 2]
    send[...] = DO[na // 2 :]
    for b in range(nb):
        blk, pos, low_at, high_at = key_at[b]
        KC[b, pl.ds(low_at, ch), :] = DL[blk, pl.ds(pos, ch), :].astype(BF)
        KC[b, pl.ds(high_at, ch), :] = DL[nkb + blk, pl.ds(pos, ch), :].astype(BF)
    dk_own[...] = KC[0]
    dk_far[...] = KC[nb - 1, own_half, :]
    dk_send[:ch] = KC[nb - 1, other_half, :]
    at = ch
    for i, o in enumerate(range(nb // 2 - 1, 0, -1)):
        mine, other = 2 * o - core, 2 * o - 1 + core
        dk[i][:ch] = KC[mine, own_half, :]
        dk[i][ch:] = KC[mine, other_half, :]
        dk_send[at : at + ch] = KC[other, other_half, :]
        dk_send[at + ch : at + tokens] = KC[other, own_half, :]
        at += tokens
    group = hd // nx
    per_core = heads // nc
    per_y = per_core // ny
    for i, j, k in itertools.product(range(nc), range(ny), range(per_y)):
        h = (core + i) % nc * per_core + (y + j) % ny * per_y + k
        cols = pl.ds(pl.multiple_of(h * hd, hd), hd)
        w = dot_tn(PK[:, cols], WA[h]).astype(BF)
        for n in range(nx):
            at = pl.multiple_of((n - x + nx) % nx * group, group)
            weights[i][j * per_y + k, pl.ds(at, group), :] = w[n * group : (n + 1) * group]


def attn_call(grid, ids, dp, ctx, packs, keys, wk, wv, wr, scaling):
    na, nb = len(packs), grid[2]
    heads, hd, dc = wk.shape
    tokens, width = keys[0].shape
    ch = tokens // 2
    per = min(4, nb)
    nkb = nb // per
    rows = heads * ch
    nc = grid[4]
    out = heads * hd + wr
    return pl.pallas_call(
        functools.partial(attn_kernel, grid, na, heads, ids.shape[1], scaling),
        in_specs=[SMEM] * 3 + [ANY] * (na + nb + 1) + [VMEM] * 2,
        out_shape=(
            (
                jax.ShapeDtypeStruct((tokens, width), BF),
                jax.ShapeDtypeStruct((ch, width), BF),
            )
            + (jax.ShapeDtypeStruct((tokens, width), BF),) * (nb // 2 - 1)
            + (jax.ShapeDtypeStruct((ch + (nb // 2 - 1) * tokens, width), BF),)
            + (jax.ShapeDtypeStruct((na // 2, tokens, out), BF),) * 2
            + (jax.ShapeDtypeStruct((heads // nc, hd, dc), BF),) * nc
        ),
        out_specs=(VMEM,) * (nb // 2 + 4 + nc),
        scratch_shapes=[
            pltpu.VMEM((na * tokens, packs[0].shape[1]), BF),
            pltpu.VMEM((nb, tokens, width), BF),
            pltpu.VMEM((na, 2, rows, width), BF),
            pltpu.VMEM((na, 2, rows, dc), BF),
            pltpu.VMEM((na, 2, rows, 128), F32),
            pltpu.VMEM((na, 2, rows, 128), F32),
            pltpu.VMEM((2 * nkb, per * ch, width), BF),
            pltpu.VMEM((2 * nkb, 8, per * ch), jnp.int32),
            pltpu.VMEM((2 * nkb, per * ch, width), F32),
            pltpu.VMEM((2, rows, width), F32),
            pltpu.VMEM((na, tokens, out), BF),
            pltpu.VMEM((heads, na * tokens, dc), BF),
            pltpu.SemaphoreType.DMA((na + nb + 1,)),
        ],
        compiler_params=vmem(44),
        cost_estimate=pl.CostEstimate(
            flops=3 * 10**10, bytes_accessed=10**7, transcendentals=10**7
        ),
        name="attn_grads",
    )(ids, dp, ctx, *packs, *keys, wk, wv)


def final_kernel(grid, heads, scale, dp_ref, ctx_ref, key_ref, mine, other, q_ref, back_ref, *refs):
    ny, nxh, nz, nxl, nc = grid
    nx = nxh * nxl
    pieces, (dqn, dqr, dlat, drope, dwk, dwv, total) = refs[:-7], refs[-7:]
    y, x, z, core = places(grid, dp_ref[0], ctx_ref[0])
    dr = drope.shape[0]
    lat = dlat.shape[1]
    ch = key_ref.shape[0] // 2
    own_half = pl.ds(pl.multiple_of(core * ch, ch), ch)
    other_half = pl.ds(pl.multiple_of((1 - core) * ch, ch), ch)
    total[...] = key_ref[...].astype(F32)
    total[own_half, :] += mine[:ch].astype(F32)
    total[other_half, :] += other[:ch].astype(F32)
    if other.shape[0] > ch:
        total[other_half, :] += mine[ch : 2 * ch].astype(F32)
        total[own_half, :] += other[ch:].astype(F32)
    key = total[...]
    dlat[...] = key[:, :lat].astype(BF)
    drope[...] = key[:, lat:].T[:dr].astype(BF)
    q = add(q_ref[0], back_ref[...])
    dqn[...] = q[:, : dqn.shape[1]]
    dqr[...] = q[:, dqn.shape[1] :]
    y, x, z, core = places(grid, dp_ref[0], ctx_ref[0])
    hd = dwk.shape[1]
    dc = dwk.shape[2]
    per_core = heads // nc
    per_y = per_core // ny
    group = hd // nx
    for i, j, n, k in itertools.product(range(nc), range(ny), range(nx), range(per_y)):
        ref = pieces[i * ny + j]
        h = (core + i) % nc * per_core + (y - j + ny) % ny * per_y + k
        at = pl.multiple_of((x - n + nx) % nx * group, group)
        r = (n * 2 * per_y + k) * group
        dwk[h, pl.ds(at, group), :] = ref[r : r + group, :].astype(F32) * scale
        r += per_y * group
        for m in range(dc // hd):
            dwv[h, pl.ds(m * hd + at, group), :] = (
                ref[r : r + group, m * hd : (m + 1) * hd].astype(F32) * scale
            )


def final_call(grid, heads, hd, dr, scale, dp, ctx, key, mine, other, q, back, pieces):
    tokens = key.shape[0]
    dc = pieces[0].shape[1]
    return pl.pallas_call(
        functools.partial(final_kernel, grid, heads, scale),
        in_specs=[SMEM, SMEM] + [VMEM] * (5 + len(pieces)),
        out_specs=(VMEM,) * 6,
        out_shape=(
            jax.ShapeDtypeStruct((tokens, heads * hd), BF),
            jax.ShapeDtypeStruct((tokens, heads * dr), BF),
            jax.ShapeDtypeStruct((tokens, dc), BF),
            jax.ShapeDtypeStruct((dr, tokens), BF),
            jax.ShapeDtypeStruct((heads, hd, dc), F32),
            jax.ShapeDtypeStruct((heads, dc, hd), F32),
        ),
        scratch_shapes=[pltpu.VMEM(key.shape, F32)],
        compiler_params=vmem(16),
        name="outputs",
    )(dp, ctx, key, mine, other, q, back, *pieces)


def make_local(grid):
    ny, nxh, nz, nxl, nc = grid
    nx = nxh * nxl

    def all_perm(x, fn):
        pairs = []
        for y, xh, z, xl, c in itertools.product(*map(range, grid)):
            y2, xh2, z2, xl2, c2 = fn(y, xh, z, xl, c)
            src = (((y * nxh + xh) * nz + z) * nxl + xl) * nc + c
            dst = (((y2 * nxh + xh2) * nz + z2) * nxl + xl2) * nc + c2
            pairs.append((src, dst))
        return lax.ppermute(x, ("dp", "ctx"), pairs)

    def z_send(x, s):
        return all_perm(x, lambda y, xh, z, xl, c: (y, xh, (z + s) % nz, xl, c))

    def z_relay(x):
        return all_perm(x, lambda y, xh, z, xl, c: (y, xh, (z + 1 - 2 * c) % nz, xl, c))

    def z_flip(x, bit):
        return all_perm(x, lambda y, xh, z, xl, c: (y, xh, z ^ bit, xl, c))

    def xl_swap(x):
        return all_perm(x, lambda y, xh, z, xl, c: (y, xh, z, nxl - 1 - xl, c))

    def c_swap(x):
        return all_perm(x, lambda y, xh, z, xl, c: (y, xh, z, xl, nc - 1 - c))

    def y_send(x, s):
        return all_perm(x, lambda y, xh, z, xl, c: ((y + s) % ny, xh, z, xl, c))

    def x_send(x, s):
        def fn(y, xh, z, xl, c):
            x2 = (xh * nxl + xl + s) % nx
            return y, x2 // nxl, z, x2 % nxl, c

        return all_perm(x, fn)

    def by_x(x, hd):
        x = x.reshape(ny, x.shape[0] // ny, nx, hd // nx, x.shape[2])
        return x.transpose(0, 2, 1, 3, 4).reshape(ny, nx, -1, x.shape[4])

    def local(span_ids, q_nope, q_rope, w_uk, latent, rope_key, w_uv, d_out, lse, saved_out):
        dp = lax.axis_index("dp").astype(jnp.int32).reshape(1)
        ctx = lax.axis_index("ctx").astype(jnp.int32).reshape(1)
        heads, hd, dc = w_uk.shape
        dr = rope_key.shape[2]
        tokens = q_nope.shape[1]
        ch = tokens // 2
        seq_rows = tokens * nz * nxl * nc
        scaling = (hd + dr) ** (-0.5)
        grad_scale = (ny * nxh * seq_rows) ** (-0.5)

        key = key_call(latent[0], rope_key[0].T)
        pack, *dwv = own_call(
            grid, dp, ctx, q_nope[0], q_rope[0], d_out[0], saved_out[0], lse[0].T, w_uv
        )

        half = nz // 2
        back, ahead = key, key
        keys = [key]
        for s in range(1, half):
            back, ahead = z_send(back, 1), z_send(ahead, -1)
            if s == 1:
                back, ahead, pack = lax.optimization_barrier((back, ahead, pack))
            else:
                back, ahead = lax.optimization_barrier((back, ahead))
            keys += [back, ahead]
        middle = back
        keys += [z_send(back[:ch], 1), z_send(ahead[ch:], -1)]

        pack_x = xl_swap(pack)
        pack_c = c_swap(pack)
        pack_x, _ = lax.optimization_barrier((pack_x, middle))
        packs = [pack, pack_x, pack_c, c_swap(pack_x)]

        dwv, dwv_send = dwv
        dwv_got = c_swap(dwv_send)
        res = attn_call(grid, span_ids, dp, ctx, packs, keys, w_uk, w_uv, heads * dr, scaling)
        dk_own, dk_far, *dk, dk_send, dq, dq_send, dwk, dwk_send = res

        t = jnp.concatenate(
            [by_x(add(dwk, c_swap(dwk_send)), hd), by_x(add(dwv, dwv_got), hd)], axis=2
        )
        t = add(t[0], *[y_send(t[s], s) for s in range(1, ny)])
        t = add(t[0], *[x_send(t[s], s) for s in range(1, nx)])
        bit = 1
        while bit < nz:
            t = add(t, z_flip(t, bit))
            bit *= 2
        t = jnp.concatenate([t] + [x_send(t, s) for s in range(1, nx)], axis=0)
        pieces = [t] + [y_send(t, s) for s in range(1, ny)]
        pieces += [c_swap(p) for p in pieces]

        dk_got = c_swap(dk_send)
        relay = z_relay(jnp.concatenate([dk_far, dk_got[:ch]], axis=0))
        at = ch
        for i, mine in enumerate(dk):
            other = dk_got[at : at + tokens]
            if i == 0:
                parts = [add(mine[:ch], relay[:ch]), mine[ch:], add(other[:ch], relay[ch:]), other[ch:]]
            else:
                parts = [add(mine, relay[:tokens]), add(other, relay[tokens:])]
            relay = z_relay(jnp.concatenate(parts, axis=0))
            at += tokens
        dk_other = c_swap(relay[relay.shape[0] // 2 :])

        q = add(dq, c_swap(dq_send))
        back = xl_swap(q[1])

        d_q_nope, d_q_rope, d_latent, d_rope_key, d_w_uk, d_w_uv = final_call(
            grid, heads, hd, dr, grad_scale, dp, ctx, dk_own, relay, dk_other, q, back, pieces
        )
        return (d_q_nope[None], d_q_rope[None], d_latent[None], d_rope_key.T[None], d_w_uk, d_w_uv)

    return local


def solution(mesh):
    dp, ctx = mesh.shape["dp"], mesh.shape["ctx"]
    grid = (dp // 2, 2, ctx // 4, 2, 2)
    rows = P("dp", "ctx", None)
    in_specs = (P("dp", None), rows, rows, P(), rows, rows, P(), rows, rows, rows)
    out_specs = (rows, rows, rows, rows, P(), P())
    return jax.shard_map(
        make_local(grid), mesh=mesh, in_specs=in_specs, out_specs=out_specs, check_vma=False
    )
```

```python
import functools
import itertools
import math

import jax
import jax.numpy as jnp
from jax import lax
from jax.experimental import pallas as pl
from jax.experimental.pallas import tpu as pltpu
from jax.sharding import PartitionSpec as P

F32 = jnp.float32
BF = jnp.bfloat16
LOG2E = math.log2(math.e)
VMEM = pl.BlockSpec(memory_space=pltpu.VMEM)
SMEM = pl.BlockSpec(memory_space=pltpu.SMEM)
ANY = pl.BlockSpec(memory_space=pl.ANY)


def vmem(mib):
    return pltpu.CompilerParams(vmem_limit_bytes=mib * 1024 * 1024)


def dot_nn(a, b):
    return lax.dot_general(a, b, (((1,), (0,)), ((), ())), preferred_element_type=F32)


def dot_nt(a, b):
    return lax.dot_general(a, b, (((1,), (1,)), ((), ())), preferred_element_type=F32)


def dot_tn(a, b):
    return lax.dot_general(a, b, (((0,), (0,)), ((), ())), preferred_element_type=F32)


def add(*terms):
    return sum(t.astype(F32) for t in terms).astype(BF)


def places(grid, dp, ctx):
    ny, nxh, nz, nxl, nc = grid
    return (
        dp // nxh,
        (dp % nxh) * nxl + (ctx // nc) % nxl,
        ctx // (nc * nxl),
        ctx % nc,
    )


def own_kernel(grid, dp_ref, ctx_ref, qn, qr, do_ref, sv_ref, lse_ref, wv_ref, pack, *dwv):
    ny, nxh, nz, nxl, nc = grid
    y, x, z, core = places(grid, dp_ref[0], ctx_ref[0])
    nx = nxh * nxl
    rows = do_ref.shape[0]
    heads, dc, hd = wv_ref.shape
    group = hd // nx
    per_core = heads // nc
    per_y = per_core // ny
    lane = lax.broadcasted_iota(jnp.int32, (rows, 128), 1)
    part = lane % (2 * heads)
    lse = lse_ref[...] * LOG2E
    gap = jnp.zeros_like(lse)
    rest = jnp.zeros((128 - 6 * heads, rows), F32)
    acc = jnp.concatenate([lse, gap, lse, gap, lse, gap, rest], axis=0).T
    for i, j, k in itertools.product(range(nc), range(ny), range(per_y)):
        h = (core + i) % nc * per_core + (y + j) % ny * per_y + k
        do = do_ref[:, pl.ds(pl.multiple_of(h * hd, hd), hd)]
        sv = sv_ref[:, pl.ds(pl.multiple_of(h * dc, dc), dc)]
        g = dot_nt(do, wv_ref[h]).astype(BF)
        delta = jnp.sum(g.astype(F32) * sv.astype(F32), axis=1, keepdims=True)
        acc = jnp.where(part == heads + h, delta, acc)
        dv = dot_tn(sv, do).astype(BF)
        for n in range(nx):
            at = pl.multiple_of((n - x + nx) % nx * group, group)
            for m in range(dc // hd):
                dwv[i][j * per_y + k, pl.ds(at, group), m * hd : (m + 1) * hd] = dv[
                    m * hd + n * group : m * hd + (n + 1) * group
                ]
    high = acc.astype(BF)
    rest = acc - high.astype(F32)
    mid = rest.astype(BF)
    low = (rest - mid.astype(F32)).astype(BF)
    wn, wr, wd = qn.shape[1], qr.shape[1], do_ref.shape[1]
    pack[:, :wn] = qn[...]
    pack[:, wn : wn + wr] = qr[...]
    pack[:, wn + wr : wn + wr + wd] = do_ref[...]
    pack[:, wn + wr + wd :] = jnp.where(
        lane < 2 * heads, high, jnp.where(lane < 4 * heads, mid, low)
    )


def own_call(grid, dp, ctx, qn, qr, do, sv, lse, wv):
    rows = do.shape[0]
    heads, dc, hd = wv.shape
    nc = grid[4]
    return pl.pallas_call(
        functools.partial(own_kernel, grid),
        in_specs=[SMEM, SMEM] + [VMEM] * 6,
        out_specs=(VMEM,) * (1 + nc),
        out_shape=(
            jax.ShapeDtypeStruct((rows, qn.shape[1] + qr.shape[1] + do.shape[1] + 128), BF),
        )
        + (jax.ShapeDtypeStruct((heads // nc, hd, dc), BF),) * nc,
        compiler_params=vmem(60),
        cost_estimate=pl.CostEstimate(flops=4 * 10**9, bytes_accessed=4 * 10**6, transcendentals=0),
        name="own_rows",
    )(dp, ctx, qn, qr, do, sv, lse, wv)


def key_kernel(lat, rope, key):
    dc = lat.shape[1]
    pad = jnp.zeros((key.shape[1] - dc - rope.shape[0], rope.shape[1]), F32)
    key[:, :dc] = lat[...]
    key[:, dc:] = jnp.concatenate([rope[...].astype(F32), pad], axis=0).T.astype(BF)


def key_call(lat, rope):
    return pl.pallas_call(
        key_kernel,
        in_specs=[VMEM] * 2,
        out_specs=VMEM,
        out_shape=jax.ShapeDtypeStruct((lat.shape[0], lat.shape[1] + 128), BF),
        compiler_params=vmem(60),
        name="key_rows",
    )(lat, rope)


def attn_kernel(grid, na, heads, spans, scaling, *refs):
    ny, nxh, nz, nxl, nc = grid
    nx = nxh * nxl
    nb = nz
    ids, dp_ref, ctx_ref = refs[:3]
    packs = refs[3 : 3 + na]
    keys = refs[3 + na : 4 + na + nb]
    wk, wv = refs[4 + na + nb : 6 + na + nb]
    out = refs[6 + na + nb :]
    n = 2 + nb // 2
    dk_own, dk_far, dk, dk_send = out[0], out[1], out[2 : n - 1], out[n - 1]
    (keep, send), weights = out[n : n + 2], out[n + 2 : n + 2 + nc]
    KC, Q, G, LB, DB, K, KP, DL, DQ, DO, WA = out[n + 2 + nc :]
    y, x, z, core = places(grid, dp_ref[0], ctx_ref[0])
    offsets = [0] + [o for s in range(1, nb // 2) for o in (-s, s)] + [nb // 2]
    xl = x % nxl

    hd, dc = wk.shape[1], wk.shape[2]
    width = K.shape[2]
    tokens = KC.shape[1]
    wn = heads * hd
    wr = DO.shape[2] - wn
    dr = wr // heads
    ch = tokens // 2
    nkb = K.shape[0] // 2
    rows = heads * ch
    per = nb // nkb
    kw = per * ch

    own_half = pl.ds(pl.multiple_of(core * ch, ch), ch)
    other_half = pl.ds(pl.multiple_of((1 - core) * ch, ch), ch)

    def first_of(z_, xl_, c_):
        return ids[0, 2 * ((z_ * nxl + xl_) * nc + c_)]

    qc = [
        first_of(z, xl, core),
        first_of(z, nxl - 1 - xl, core),
        first_of(z, xl, nc - 1 - core),
        first_of(z, nxl - 1 - xl, nc - 1 - core),
    ][:na]
    kc = [first_of((z + o + nz) % nz, xl, core) for o in offsets]

    def low_span(c):
        return jnp.minimum(c, spans - 1 - c)

    klow = [low_span(c) for c in kc]
    slots = [sum(jnp.where(other < mine, 1, 0) for other in klow) for mine in klow]

    def pick(values, a):
        out = values[0]
        for i in range(1, len(values)):
            out = jnp.where(a == i, values[i], out)
        return out

    DL[...] = jnp.zeros_like(DL)


    lows = [jnp.where(2 * c < spans, 0, 1) for c in qc]
    for a in range(na):
        stats = packs[a][:, wn + wr + wn :].astype(F32)
        stats = (
            stats[:, : 2 * heads] + stats[:, 2 * heads : 4 * heads] + stats[:, 4 * heads : 6 * heads]
        )
        for h in range(heads):
            ql = dot_nn(packs[a][:, h * hd : (h + 1) * hd], wk[h]).astype(BF)
            gl = dot_nt(packs[a][:, wn + wr + h * hd : wn + wr + (h + 1) * hd], wv[h]).astype(BF)
            qrot = packs[a][:, wn + h * dr : wn + (h + 1) * dr]
            to = slice(h * ch, (h + 1) * ch)
            for slot in range(2):
                mine = slice(slot * ch, (slot + 1) * ch)
                half = lows[a] if slot == 0 else 1 - lows[a]
                Q[a, half, to, :dc] = ql[mine]
                Q[a, half, to, dc : dc + dr] = qrot[mine]
                Q[a, half, to, dc + dr :] = jnp.zeros((ch, width - dc - dr), BF)
                G[a, half, to, :] = gl[mine]
                LB[a, half, to, :] = jnp.broadcast_to(stats[mine, h : h + 1], (ch, 128))
                DB[a, half, to, :] = jnp.broadcast_to(
                    stats[mine, heads + h : heads + h + 1], (ch, 128)
                )

    lane = lax.broadcasted_iota(jnp.int32, (8, kw), 1)
    kps = [jnp.zeros((8, kw), jnp.int32) for _ in range(2 * nkb)]
    key_at = []
    for b in range(nb):
        blk = slots[b] // per
        pos = pl.multiple_of((slots[b] % per) * ch, ch)
        first = 2 * kc[b] < spans
        low_at = pl.multiple_of(jnp.where(first, 0, ch), ch)
        high_at = pl.multiple_of(jnp.where(first, ch, 0), ch)
        key_at.append((blk, pos, low_at, high_at))
        if b < nb - 1:
            low_rows, high_rows = keys[b][pl.ds(low_at, ch), :], keys[b][pl.ds(high_at, ch), :]
        else:
            low_rows = jnp.where(first, keys[nb - 1][...], keys[nb][...])
            high_rows = jnp.where(first, keys[nb][...], keys[nb - 1][...])
        K[blk, pl.ds(pos, ch), :] = low_rows
        K[nkb + blk, pl.ds(pos, ch), :] = high_rows
        inside = jnp.logical_and(lane >= pos, lane < pos + ch)
        for i in range(nkb):
            here = jnp.logical_and(inside, blk == i)
            kps[i] = jnp.where(here, klow[b] * ch + (lane - pos), kps[i])
            kps[nkb + i] = jnp.where(here, (spans - 1 - klow[b]) * ch + (lane - pos), kps[nkb + i])
    for i in range(2 * nkb):
        KP[i] = kps[i]

    sub = min(rows, 256)
    wide = kw // 128
    qtok = lax.broadcasted_iota(jnp.int32, (sub, kw), 0) % ch

    def unit(a, half, kb, span, fresh):
        kpos = KP[kb][0:1, :]

        def scores(r):
            rr = slice(r * sub, (r + 1) * sub)
            return dot_nt(Q[a, half, rr, :], K[kb]), dot_nt(G[a, half, rr, :], K[kb, :, :dc])

        dss, pbs = [], []
        ready = scores(0)
        for r in range(rows // sub):
            rr = slice(r * sub, (r + 1) * sub)
            s, dp = ready
            if r + 1 < rows // sub:
                ready = scores(r + 1)
            lb = jnp.concatenate([LB[a, half, rr, :]] * wide, axis=1)
            db = jnp.concatenate([DB[a, half, rr, :]] * wide, axis=1)
            p = jnp.exp2(s * (scaling * LOG2E) - lb)
            p = jnp.where(kpos <= span * ch + qtok, p, 0.0)
            dss.append((p * ((dp - db) * scaling)).astype(BF))
            pbs.append(p.astype(BF))
        ds = jnp.concatenate(dss, axis=0)
        pb = jnp.concatenate(pbs, axis=0)
        DQ[half] = jnp.where(fresh, 0.0, DQ[half]) + dot_nn(ds, K[kb])
        DL[kb, :, :dc] += dot_tn(pb, G[a, half]) + dot_tn(ds, Q[a, half, :, :dc])
        DL[kb, :, dc:] += dot_tn(ds, Q[a, half, :, dc:])

    def query_set(a, _):
        c = pick(qc, a)
        lo = low_span(c)
        hi = spans - 1 - lo
        below = sum(jnp.where(k <= lo, 1, 0) for k in klow)
        above = sum(jnp.where(k >= lo, 1, 0) for k in klow)

        @pl.when(below == 0)
        def _():
            DQ[0] = jnp.zeros_like(DQ[0])


        def step(u, _):
            blk = u // 3
            kind = u % 3
            half = jnp.where(kind == 1, 0, 1)
            kb = jnp.where(kind == 2, nkb + blk, blk)
            need = jnp.where(
                kind == 1, below > per * blk, jnp.where(kind == 2, nb - above < per * (blk + 1), True)
            )

            @pl.when(need)
            def _():
                unit(a, half, kb, jnp.where(kind == 1, lo, hi), u < 2)

            return 0

        lax.fori_loop(0, 3 * nkb, step, 0)

        low = jnp.where(2 * c < spans, 0, 1)
        for h in range(heads):
            to = slice(h * ch, (h + 1) * ch)
            d = jnp.concatenate([DQ[low, to, :], DQ[1 - low, to, :]], axis=0).astype(BF)
            DO[a, :, wn + h * dr : wn + (h + 1) * dr] = d[:, dc : dc + dr]
            WA[h, pl.ds(pl.multiple_of(a * tokens, tokens), tokens), :] = d[:, :dc]
        return 0

    lax.fori_loop(0, na, query_set, 0)

    for h in range(heads):
        d = dot_nt(WA[h], wk[h]).astype(BF)
        for a in range(na):
            DO[a, :, h * hd : (h + 1) * hd] = d[a * tokens : (a + 1) * tokens]
    keep[...] = DO[: na // 2]
    send[...] = DO[na // 2 :]
    for b in range(nb):
        blk, pos, low_at, high_at = key_at[b]
        KC[b, pl.ds(low_at, ch), :] = DL[blk, pl.ds(pos, ch), :].astype(BF)
        KC[b, pl.ds(high_at, ch), :] = DL[nkb + blk, pl.ds(pos, ch), :].astype(BF)
    dk_own[...] = KC[0]
    dk_far[...] = KC[nb - 1, own_half, :]
    dk_send[:ch] = KC[nb - 1, other_half, :]
    at = ch
    for i, o in enumerate(range(nb // 2 - 1, 0, -1)):
        mine, other = 2 * o - core, 2 * o - 1 + core
        dk[i][:ch] = KC[mine, own_half, :]
        dk[i][ch:] = KC[mine, other_half, :]
        dk_send[at : at + ch] = KC[other, other_half, :]
        dk_send[at + ch : at + tokens] = KC[other, own_half, :]
        at += tokens
    group = hd // nx
    per_core = heads // nc
    per_y = per_core // ny
    for i, j, k in itertools.product(range(nc), range(ny), range(per_y)):
        h = (core + i) % nc * per_core + (y + j) % ny * per_y + k
        cols = pl.ds(pl.multiple_of(h * hd, hd), hd)
        w = sum(
            dot_tn(packs[a][:, cols], WA[h, a * tokens : (a + 1) * tokens, :]) for a in range(na)
        ).astype(BF)
        for n in range(nx):
            at = pl.multiple_of((n - x + nx) % nx * group, group)
            weights[i][j * per_y + k, pl.ds(at, group), :] = w[n * group : (n + 1) * group]


def attn_call(grid, ids, dp, ctx, packs, keys, wk, wv, wr, scaling):
    na, nb = len(packs), grid[2]
    heads, hd, dc = wk.shape
    tokens, width = keys[0].shape
    ch = tokens // 2
    per = min(4, nb)
    nkb = nb // per
    rows = heads * ch
    nc = grid[4]
    out = heads * hd + wr
    return pl.pallas_call(
        functools.partial(attn_kernel, grid, na, heads, ids.shape[1], scaling),
        in_specs=[SMEM] * 3 + [VMEM] * (na + nb + 3),
        out_shape=(
            (
                jax.ShapeDtypeStruct((tokens, width), BF),
                jax.ShapeDtypeStruct((ch, width), BF),
            )
            + (jax.ShapeDtypeStruct((tokens, width), BF),) * (nb // 2 - 1)
            + (jax.ShapeDtypeStruct((ch + (nb // 2 - 1) * tokens, width), BF),)
            + (jax.ShapeDtypeStruct((na // 2, tokens, out), BF),) * 2
            + (jax.ShapeDtypeStruct((heads // nc, hd, dc), BF),) * nc
        ),
        out_specs=(VMEM,) * (nb // 2 + 4 + nc),
        scratch_shapes=[
            pltpu.VMEM((nb, tokens, width), BF),
            pltpu.VMEM((na, 2, rows, width), BF),
            pltpu.VMEM((na, 2, rows, dc), BF),
            pltpu.VMEM((na, 2, rows, 128), F32),
            pltpu.VMEM((na, 2, rows, 128), F32),
            pltpu.VMEM((2 * nkb, per * ch, width), BF),
            pltpu.VMEM((2 * nkb, 8, per * ch), jnp.int32),
            pltpu.VMEM((2 * nkb, per * ch, width), F32),
            pltpu.VMEM((2, rows, width), F32),
            pltpu.VMEM((na, tokens, out), BF),
            pltpu.VMEM((heads, na * tokens, dc), BF),
        ],
        compiler_params=vmem(44),
        cost_estimate=pl.CostEstimate(
            flops=3 * 10**10, bytes_accessed=10**7, transcendentals=10**7
        ),
        name="attn_grads",
    )(ids, dp, ctx, *packs, *keys, wk, wv)


def final_kernel(grid, heads, scale, dp_ref, ctx_ref, key_ref, mine, other, q_ref, back_ref, *refs):
    ny, nxh, nz, nxl, nc = grid
    nx = nxh * nxl
    pieces, (dqn, dqr, dlat, drope, dwk, dwv, total) = refs[:-7], refs[-7:]
    y, x, z, core = places(grid, dp_ref[0], ctx_ref[0])
    dr = drope.shape[0]
    lat = dlat.shape[1]
    ch = key_ref.shape[0] // 2
    own_half = pl.ds(pl.multiple_of(core * ch, ch), ch)
    other_half = pl.ds(pl.multiple_of((1 - core) * ch, ch), ch)
    total[...] = key_ref[...].astype(F32)
    total[own_half, :] += mine[:ch].astype(F32)
    total[other_half, :] += other[:ch].astype(F32)
    if other.shape[0] > ch:
        total[other_half, :] += mine[ch : 2 * ch].astype(F32)
        total[own_half, :] += other[ch:].astype(F32)
    key = total[...]
    dlat[...] = key[:, :lat].astype(BF)
    drope[...] = key[:, lat:].T[:dr].astype(BF)
    q = add(q_ref[0], back_ref[...])
    dqn[...] = q[:, : dqn.shape[1]]
    dqr[...] = q[:, dqn.shape[1] :]
    y, x, z, core = places(grid, dp_ref[0], ctx_ref[0])
    hd = dwk.shape[1]
    dc = dwk.shape[2]
    per_core = heads // nc
    per_y = per_core // ny
    group = hd // nx
    for i, j, n, k in itertools.product(range(nc), range(ny), range(nx), range(per_y)):
        ref = pieces[i * ny + j]
        h = (core + i) % nc * per_core + (y - j + ny) % ny * per_y + k
        at = pl.multiple_of((x - n + nx) % nx * group, group)
        r = (n * 2 * per_y + k) * group
        dwk[h, pl.ds(at, group), :] = ref[r : r + group, :].astype(F32) * scale
        r += per_y * group
        for m in range(dc // hd):
            dwv[h, pl.ds(m * hd + at, group), :] = (
                ref[r : r + group, m * hd : (m + 1) * hd].astype(F32) * scale
            )


def final_call(grid, heads, hd, dr, scale, dp, ctx, key, mine, other, q, back, pieces):
    tokens = key.shape[0]
    dc = pieces[0].shape[1]
    return pl.pallas_call(
        functools.partial(final_kernel, grid, heads, scale),
        in_specs=[SMEM, SMEM] + [VMEM] * (5 + len(pieces)),
        out_specs=(VMEM,) * 6,
        out_shape=(
            jax.ShapeDtypeStruct((tokens, heads * hd), BF),
            jax.ShapeDtypeStruct((tokens, heads * dr), BF),
            jax.ShapeDtypeStruct((tokens, dc), BF),
            jax.ShapeDtypeStruct((dr, tokens), BF),
            jax.ShapeDtypeStruct((heads, hd, dc), F32),
            jax.ShapeDtypeStruct((heads, dc, hd), F32),
        ),
        scratch_shapes=[pltpu.VMEM(key.shape, F32)],
        compiler_params=vmem(16),
        name="outputs",
    )(dp, ctx, key, mine, other, q, back, *pieces)


def make_local(grid):
    ny, nxh, nz, nxl, nc = grid
    nx = nxh * nxl

    def all_perm(x, fn):
        pairs = []
        for y, xh, z, xl, c in itertools.product(*map(range, grid)):
            y2, xh2, z2, xl2, c2 = fn(y, xh, z, xl, c)
            src = (((y * nxh + xh) * nz + z) * nxl + xl) * nc + c
            dst = (((y2 * nxh + xh2) * nz + z2) * nxl + xl2) * nc + c2
            pairs.append((src, dst))
        return lax.ppermute(x, ("dp", "ctx"), pairs)

    def z_send(x, s):
        return all_perm(x, lambda y, xh, z, xl, c: (y, xh, (z + s) % nz, xl, c))

    def z_relay(x):
        return all_perm(x, lambda y, xh, z, xl, c: (y, xh, (z + 1 - 2 * c) % nz, xl, c))

    def z_flip(x, bit):
        return all_perm(x, lambda y, xh, z, xl, c: (y, xh, z ^ bit, xl, c))

    def xl_swap(x):
        return all_perm(x, lambda y, xh, z, xl, c: (y, xh, z, nxl - 1 - xl, c))

    def c_swap(x):
        return all_perm(x, lambda y, xh, z, xl, c: (y, xh, z, xl, nc - 1 - c))

    def y_send(x, s):
        return all_perm(x, lambda y, xh, z, xl, c: ((y + s) % ny, xh, z, xl, c))

    def x_send(x, s):
        def fn(y, xh, z, xl, c):
            x2 = (xh * nxl + xl + s) % nx
            return y, x2 // nxl, z, x2 % nxl, c

        return all_perm(x, fn)

    def by_x(x, hd):
        x = x.reshape(ny, x.shape[0] // ny, nx, hd // nx, x.shape[2])
        return x.transpose(0, 2, 1, 3, 4).reshape(ny, nx, -1, x.shape[4])

    def local(span_ids, q_nope, q_rope, w_uk, latent, rope_key, w_uv, d_out, lse, saved_out):
        dp = lax.axis_index("dp").astype(jnp.int32).reshape(1)
        ctx = lax.axis_index("ctx").astype(jnp.int32).reshape(1)
        heads, hd, dc = w_uk.shape
        dr = rope_key.shape[2]
        tokens = q_nope.shape[1]
        ch = tokens // 2
        seq_rows = tokens * nz * nxl * nc
        scaling = (hd + dr) ** (-0.5)
        grad_scale = (ny * nxh * seq_rows) ** (-0.5)

        key = key_call(latent[0], rope_key[0].T)
        pack, *dwv = own_call(
            grid, dp, ctx, q_nope[0], q_rope[0], d_out[0], saved_out[0], lse[0].T, w_uv
        )

        half = nz // 2
        back, ahead = key, key
        keys = [key]
        for s in range(1, half):
            back, ahead = z_send(back, 1), z_send(ahead, -1)
            if s == 1:
                back, ahead, pack = lax.optimization_barrier((back, ahead, pack))
            else:
                back, ahead = lax.optimization_barrier((back, ahead))
            keys += [back, ahead]
        middle = back
        keys += [z_send(back[:ch], 1), z_send(ahead[ch:], -1)]

        pack_x = xl_swap(pack)
        pack_c = c_swap(pack)
        pack_x, _ = lax.optimization_barrier((pack_x, middle))
        packs = [pack, pack_x, pack_c, c_swap(pack_x)]

        dwv, dwv_send = dwv
        dwv_got = c_swap(dwv_send)
        res = attn_call(grid, span_ids, dp, ctx, packs, keys, w_uk, w_uv, heads * dr, scaling)
        dk_own, dk_far, *dk, dk_send, dq, dq_send, dwk, dwk_send = res

        t = jnp.concatenate(
            [by_x(add(dwk, c_swap(dwk_send)), hd), by_x(add(dwv, dwv_got), hd)], axis=2
        )
        t = add(t[0], *[y_send(t[s], s) for s in range(1, ny)])
        t = add(t[0], *[x_send(t[s], s) for s in range(1, nx)])
        bit = 1
        while bit < nz:
            t = add(t, z_flip(t, bit))
            bit *= 2
        t = jnp.concatenate([t] + [x_send(t, s) for s in range(1, nx)], axis=0)
        pieces = [t] + [y_send(t, s) for s in range(1, ny)]
        pieces += [c_swap(p) for p in pieces]

        dk_got = c_swap(dk_send)
        relay = z_relay(jnp.concatenate([dk_far, dk_got[:ch]], axis=0))
        at = ch
        for i, mine in enumerate(dk):
            other = dk_got[at : at + tokens]
            if i == 0:
                parts = [add(mine[:ch], relay[:ch]), mine[ch:], add(other[:ch], relay[ch:]), other[ch:]]
            else:
                parts = [add(mine, relay[:tokens]), add(other, relay[tokens:])]
            relay = z_relay(jnp.concatenate(parts, axis=0))
            at += tokens
        dk_other = c_swap(relay[relay.shape[0] // 2 :])

        q = add(dq, c_swap(dq_send))
        back = xl_swap(q[1])

        d_q_nope, d_q_rope, d_latent, d_rope_key, d_w_uk, d_w_uv = final_call(
            grid, heads, hd, dr, grad_scale, dp, ctx, dk_own, relay, dk_other, q, back, pieces
        )
        return (d_q_nope[None], d_q_rope[None], d_latent[None], d_rope_key.T[None], d_w_uk, d_w_uv)

    return local


def solution(mesh):
    dp, ctx = mesh.shape["dp"], mesh.shape["ctx"]
    grid = (dp // 2, 2, ctx // 4, 2, 2)
    rows = P("dp", "ctx", None)
    in_specs = (P("dp", None), rows, rows, P(), rows, rows, P(), rows, rows, rows)
    out_specs = (rows, rows, rows, rows, P(), P())
    return jax.shard_map(
        make_local(grid), mesh=mesh, in_specs=in_specs, out_specs=out_specs, check_vma=False
    )
```

```python
import functools
import itertools
import math

import jax
import jax.numpy as jnp
from jax import lax
from jax.experimental import pallas as pl
from jax.experimental.pallas import tpu as pltpu
from jax.sharding import PartitionSpec as P

F32 = jnp.float32
BF = jnp.bfloat16
LOG2E = math.log2(math.e)
VMEM = pl.BlockSpec(memory_space=pltpu.VMEM)
SMEM = pl.BlockSpec(memory_space=pltpu.SMEM)
ANY = pl.BlockSpec(memory_space=pl.ANY)


def vmem(mib):
    return pltpu.CompilerParams(vmem_limit_bytes=mib * 1024 * 1024)


def dot_nn(a, b):
    return lax.dot_general(a, b, (((1,), (0,)), ((), ())), preferred_element_type=F32)


def dot_nt(a, b):
    return lax.dot_general(a, b, (((1,), (1,)), ((), ())), preferred_element_type=F32)


def dot_tn(a, b):
    return lax.dot_general(a, b, (((0,), (0,)), ((), ())), preferred_element_type=F32)


def add(*terms):
    return sum(t.astype(F32) for t in terms).astype(BF)


def places(grid, dp, ctx):
    ny, nxh, nz, nxl, nc = grid
    return (
        dp // nxh,
        (dp % nxh) * nxl + (ctx // nc) % nxl,
        ctx // (nc * nxl),
        ctx % nc,
    )


def own_kernel(grid, dp_ref, ctx_ref, qn, qr, do_ref, sv_ref, lse_ref, wv_ref, pack, *dwv):
    ny, nxh, nz, nxl, nc = grid
    y, x, z, core = places(grid, dp_ref[0], ctx_ref[0])
    nx = nxh * nxl
    rows = do_ref.shape[0]
    heads, dc, hd = wv_ref.shape
    group = hd // nx
    per_core = heads // nc
    per_y = per_core // ny
    lane = lax.broadcasted_iota(jnp.int32, (rows, 128), 1)
    part = lane % (2 * heads)
    lse = lse_ref[...] * LOG2E
    gap = jnp.zeros_like(lse)
    rest = jnp.zeros((128 - 6 * heads, rows), F32)
    acc = jnp.concatenate([lse, gap, lse, gap, lse, gap, rest], axis=0).T
    for i, j, k in itertools.product(range(nc), range(ny), range(per_y)):
        h = (core + i) % nc * per_core + (y + j) % ny * per_y + k
        do = do_ref[:, pl.ds(pl.multiple_of(h * hd, hd), hd)]
        sv = sv_ref[:, pl.ds(pl.multiple_of(h * dc, dc), dc)]
        g = dot_nt(do, wv_ref[h]).astype(BF)
        delta = jnp.sum(g.astype(F32) * sv.astype(F32), axis=1, keepdims=True)
        acc = jnp.where(part == heads + h, delta, acc)
        dv = dot_tn(sv, do).astype(BF)
        for n in range(nx):
            at = pl.multiple_of((n - x + nx) % nx * group, group)
            for m in range(dc // hd):
                dwv[i][j * per_y + k, pl.ds(at, group), m * hd : (m + 1) * hd] = dv[
                    m * hd + n * group : m * hd + (n + 1) * group
                ]
    high = acc.astype(BF)
    rest = acc - high.astype(F32)
    mid = rest.astype(BF)
    low = (rest - mid.astype(F32)).astype(BF)
    wn, wr, wd = qn.shape[1], qr.shape[1], do_ref.shape[1]
    pack[:, :wn] = qn[...]
    pack[:, wn : wn + wr] = qr[...]
    pack[:, wn + wr : wn + wr + wd] = do_ref[...]
    pack[:, wn + wr + wd :] = jnp.where(
        lane < 2 * heads, high, jnp.where(lane < 4 * heads, mid, low)
    )


def own_call(grid, dp, ctx, qn, qr, do, sv, lse, wv):
    rows = do.shape[0]
    heads, dc, hd = wv.shape
    nc = grid[4]
    return pl.pallas_call(
        functools.partial(own_kernel, grid),
        in_specs=[SMEM, SMEM] + [VMEM] * 6,
        out_specs=(VMEM,) * (1 + nc),
        out_shape=(
            pltpu.VMEM((rows, qn.shape[1] + qr.shape[1] + do.shape[1] + 128), BF),
        )
        + (jax.ShapeDtypeStruct((heads // nc, hd, dc), BF),) * nc,
        compiler_params=vmem(60),
        cost_estimate=pl.CostEstimate(flops=4 * 10**9, bytes_accessed=4 * 10**6, transcendentals=0),
        name="own_rows",
    )(dp, ctx, qn, qr, do, sv, lse, wv)


def key_kernel(lat, rope, key):
    dc = lat.shape[1]
    pad = jnp.zeros((key.shape[1] - dc - rope.shape[0], rope.shape[1]), F32)
    key[:, :dc] = lat[...]
    key[:, dc:] = jnp.concatenate([rope[...].astype(F32), pad], axis=0).T.astype(BF)


def key_call(lat, rope):
    return pl.pallas_call(
        key_kernel,
        in_specs=[VMEM] * 2,
        out_specs=VMEM,
        out_shape=jax.ShapeDtypeStruct((lat.shape[0], lat.shape[1] + 128), BF),
        compiler_params=vmem(60),
        name="key_rows",
    )(lat, rope)


def attn_kernel(grid, na, heads, spans, scaling, *refs):
    ny, nxh, nz, nxl, nc = grid
    nx = nxh * nxl
    nb = nz
    ids, dp_ref, ctx_ref = refs[:3]
    packs = refs[3 : 3 + na]
    keys = refs[3 + na : 4 + na + nb]
    wk, wv = refs[4 + na + nb : 6 + na + nb]
    out = refs[6 + na + nb :]
    n = 2 + nb // 2
    dk_own, dk_far, dk, dk_send = out[0], out[1], out[2 : n - 1], out[n - 1]
    (keep, send), weights = out[n : n + 2], out[n + 2 : n + 2 + nc]
    KC, Q, G, LB, DB, K, KP, DL, DQ, DO, WA = out[n + 2 + nc :]
    y, x, z, core = places(grid, dp_ref[0], ctx_ref[0])
    offsets = [0] + [o for s in range(1, nb // 2) for o in (-s, s)] + [nb // 2]
    xl = x % nxl

    hd, dc = wk.shape[1], wk.shape[2]
    width = K.shape[2]
    tokens = KC.shape[1]
    wn = heads * hd
    wr = DO.shape[2] - wn
    dr = wr // heads
    ch = tokens // 2
    nkb = K.shape[0] // 2
    rows = heads * ch
    per = nb // nkb
    kw = per * ch

    own_half = pl.ds(pl.multiple_of(core * ch, ch), ch)
    other_half = pl.ds(pl.multiple_of((1 - core) * ch, ch), ch)

    def first_of(z_, xl_, c_):
        return ids[0, 2 * ((z_ * nxl + xl_) * nc + c_)]

    qc = [
        first_of(z, xl, core),
        first_of(z, nxl - 1 - xl, core),
        first_of(z, xl, nc - 1 - core),
        first_of(z, nxl - 1 - xl, nc - 1 - core),
    ][:na]
    kc = [first_of((z + o + nz) % nz, xl, core) for o in offsets]

    def low_span(c):
        return jnp.minimum(c, spans - 1 - c)

    klow = [low_span(c) for c in kc]
    slots = [sum(jnp.where(other < mine, 1, 0) for other in klow) for mine in klow]

    def pick(values, a):
        out = values[0]
        for i in range(1, len(values)):
            out = jnp.where(a == i, values[i], out)
        return out

    DL[...] = jnp.zeros_like(DL)


    lows = [jnp.where(2 * c < spans, 0, 1) for c in qc]
    for a in range(na):
        stats = packs[a][:, wn + wr + wn :].astype(F32)
        stats = (
            stats[:, : 2 * heads] + stats[:, 2 * heads : 4 * heads] + stats[:, 4 * heads : 6 * heads]
        )
        for h in range(heads):
            ql = dot_nn(packs[a][:, h * hd : (h + 1) * hd], wk[h]).astype(BF)
            gl = dot_nt(packs[a][:, wn + wr + h * hd : wn + wr + (h + 1) * hd], wv[h]).astype(BF)
            qrot = packs[a][:, wn + h * dr : wn + (h + 1) * dr]
            to = slice(h * ch, (h + 1) * ch)
            for slot in range(2):
                mine = slice(slot * ch, (slot + 1) * ch)
                half = lows[a] if slot == 0 else 1 - lows[a]
                Q[a, half, to, :dc] = ql[mine]
                Q[a, half, to, dc : dc + dr] = qrot[mine]
                Q[a, half, to, dc + dr :] = jnp.zeros((ch, width - dc - dr), BF)
                G[a, half, to, :] = gl[mine]
                LB[a, half, to, :] = jnp.broadcast_to(stats[mine, h : h + 1], (ch, 128))
                DB[a, half, to, :] = jnp.broadcast_to(
                    stats[mine, heads + h : heads + h + 1], (ch, 128)
                )

    lane = lax.broadcasted_iota(jnp.int32, (8, kw), 1)
    kps = [jnp.zeros((8, kw), jnp.int32) for _ in range(2 * nkb)]
    key_at = []
    for b in range(nb):
        blk = slots[b] // per
        pos = pl.multiple_of((slots[b] % per) * ch, ch)
        first = 2 * kc[b] < spans
        low_at = pl.multiple_of(jnp.where(first, 0, ch), ch)
        high_at = pl.multiple_of(jnp.where(first, ch, 0), ch)
        key_at.append((blk, pos, low_at, high_at))
        if b < nb - 1:
            low_rows, high_rows = keys[b][pl.ds(low_at, ch), :], keys[b][pl.ds(high_at, ch), :]
        else:
            low_rows = jnp.where(first, keys[nb - 1][...], keys[nb][...])
            high_rows = jnp.where(first, keys[nb][...], keys[nb - 1][...])
        K[blk, pl.ds(pos, ch), :] = low_rows
        K[nkb + blk, pl.ds(pos, ch), :] = high_rows
        inside = jnp.logical_and(lane >= pos, lane < pos + ch)
        for i in range(nkb):
            here = jnp.logical_and(inside, blk == i)
            kps[i] = jnp.where(here, klow[b] * ch + (lane - pos), kps[i])
            kps[nkb + i] = jnp.where(here, (spans - 1 - klow[b]) * ch + (lane - pos), kps[nkb + i])
    for i in range(2 * nkb):
        KP[i] = kps[i]

    sub = min(rows, 256)
    wide = kw // 128
    qtok = lax.broadcasted_iota(jnp.int32, (sub, kw), 0) % ch

    def unit(a, half, kb, span, fresh):
        kpos = KP[kb][0:1, :]

        def scores(r):
            rr = slice(r * sub, (r + 1) * sub)
            return dot_nt(Q[a, half, rr, :], K[kb]), dot_nt(G[a, half, rr, :], K[kb, :, :dc])

        dss, pbs = [], []
        ready = scores(0)
        for r in range(rows // sub):
            rr = slice(r * sub, (r + 1) * sub)
            s, dp = ready
            if r + 1 < rows // sub:
                ready = scores(r + 1)
            lb = jnp.concatenate([LB[a, half, rr, :]] * wide, axis=1)
            db = jnp.concatenate([DB[a, half, rr, :]] * wide, axis=1)
            p = jnp.exp2(s * (scaling * LOG2E) - lb)
            p = jnp.where(kpos <= span * ch + qtok, p, 0.0)
            dss.append((p * ((dp - db) * scaling)).astype(BF))
            pbs.append(p.astype(BF))
        ds = jnp.concatenate(dss, axis=0)
        pb = jnp.concatenate(pbs, axis=0)
        DQ[half] = jnp.where(fresh, 0.0, DQ[half]) + dot_nn(ds, K[kb])
        DL[kb, :, :dc] += dot_tn(pb, G[a, half]) + dot_tn(ds, Q[a, half, :, :dc])
        DL[kb, :, dc:] += dot_tn(ds, Q[a, half, :, dc:])

    def query_set(a, _):
        c = pick(qc, a)
        lo = low_span(c)
        hi = spans - 1 - lo
        below = sum(jnp.where(k <= lo, 1, 0) for k in klow)
        above = sum(jnp.where(k >= lo, 1, 0) for k in klow)

        @pl.when(below == 0)
        def _():
            DQ[0] = jnp.zeros_like(DQ[0])


        def step(u, _):
            blk = u // 3
            kind = u % 3
            half = jnp.where(kind == 1, 0, 1)
            kb = jnp.where(kind == 2, nkb + blk, blk)
            need = jnp.where(
                kind == 1, below > per * blk, jnp.where(kind == 2, nb - above < per * (blk + 1), True)
            )

            @pl.when(need)
            def _():
                unit(a, half, kb, jnp.where(kind == 1, lo, hi), u < 2)

            return 0

        lax.fori_loop(0, 3 * nkb, step, 0)

        low = jnp.where(2 * c < spans, 0, 1)
        for h in range(heads):
            to = slice(h * ch, (h + 1) * ch)
            d = jnp.concatenate([DQ[low, to, :], DQ[1 - low, to, :]], axis=0).astype(BF)
            DO[a, :, wn + h * dr : wn + (h + 1) * dr] = d[:, dc : dc + dr]
            WA[h, pl.ds(pl.multiple_of(a * tokens, tokens), tokens), :] = d[:, :dc]
        return 0

    lax.fori_loop(0, na, query_set, 0)

    for h in range(heads):
        d = dot_nt(WA[h], wk[h]).astype(BF)
        for a in range(na):
            DO[a, :, h * hd : (h + 1) * hd] = d[a * tokens : (a + 1) * tokens]
    keep[...] = DO[: na // 2]
    send[...] = DO[na // 2 :]
    for b in range(nb):
        blk, pos, low_at, high_at = key_at[b]
        KC[b, pl.ds(low_at, ch), :] = DL[blk, pl.ds(pos, ch), :].astype(BF)
        KC[b, pl.ds(high_at, ch), :] = DL[nkb + blk, pl.ds(pos, ch), :].astype(BF)
    dk_own[...] = KC[0]
    dk_far[...] = KC[nb - 1, own_half, :]
    dk_send[:ch] = KC[nb - 1, other_half, :]
    at = ch
    for i, o in enumerate(range(nb // 2 - 1, 0, -1)):
        mine, other = 2 * o - core, 2 * o - 1 + core
        dk[i][:ch] = KC[mine, own_half, :]
        dk[i][ch:] = KC[mine, other_half, :]
        dk_send[at : at + ch] = KC[other, other_half, :]
        dk_send[at + ch : at + tokens] = KC[other, own_half, :]
        at += tokens
    group = hd // nx
    per_core = heads // nc
    per_y = per_core // ny
    for i, j, k in itertools.product(range(nc), range(ny), range(per_y)):
        h = (core + i) % nc * per_core + (y + j) % ny * per_y + k
        cols = pl.ds(pl.multiple_of(h * hd, hd), hd)
        w = sum(
            dot_tn(packs[a][:, cols], WA[h, a * tokens : (a + 1) * tokens, :]) for a in range(na)
        ).astype(BF)
        for n in range(nx):
            at = pl.multiple_of((n - x + nx) % nx * group, group)
            weights[i][j * per_y + k, pl.ds(at, group), :] = w[n * group : (n + 1) * group]


def attn_call(grid, ids, dp, ctx, packs, keys, wk, wv, wr, scaling):
    na, nb = len(packs), grid[2]
    heads, hd, dc = wk.shape
    tokens, width = keys[0].shape
    ch = tokens // 2
    per = min(4, nb)
    nkb = nb // per
    rows = heads * ch
    nc = grid[4]
    out = heads * hd + wr
    return pl.pallas_call(
        functools.partial(attn_kernel, grid, na, heads, ids.shape[1], scaling),
        in_specs=[SMEM] * 3 + [VMEM] * (na + nb + 3),
        out_shape=(
            (
                jax.ShapeDtypeStruct((tokens, width), BF),
                jax.ShapeDtypeStruct((ch, width), BF),
            )
            + (jax.ShapeDtypeStruct((tokens, width), BF),) * (nb // 2 - 1)
            + (jax.ShapeDtypeStruct((ch + (nb // 2 - 1) * tokens, width), BF),)
            + (jax.ShapeDtypeStruct((na // 2, tokens, out), BF),) * 2
            + (jax.ShapeDtypeStruct((heads // nc, hd, dc), BF),) * nc
        ),
        out_specs=(VMEM,) * (nb // 2 + 4 + nc),
        scratch_shapes=[
            pltpu.VMEM((nb, tokens, width), BF),
            pltpu.VMEM((na, 2, rows, width), BF),
            pltpu.VMEM((na, 2, rows, dc), BF),
            pltpu.VMEM((na, 2, rows, 128), F32),
            pltpu.VMEM((na, 2, rows, 128), F32),
            pltpu.VMEM((2 * nkb, per * ch, width), BF),
            pltpu.VMEM((2 * nkb, 8, per * ch), jnp.int32),
            pltpu.VMEM((2 * nkb, per * ch, width), F32),
            pltpu.VMEM((2, rows, width), F32),
            pltpu.VMEM((na, tokens, out), BF),
            pltpu.VMEM((heads, na * tokens, dc), BF),
        ],
        compiler_params=vmem(44),
        cost_estimate=pl.CostEstimate(
            flops=3 * 10**10, bytes_accessed=10**7, transcendentals=10**7
        ),
        name="attn_grads",
    )(ids, dp, ctx, *packs, *keys, wk, wv)


def final_kernel(grid, heads, scale, dp_ref, ctx_ref, key_ref, mine, other, q_ref, back_ref, *refs):
    ny, nxh, nz, nxl, nc = grid
    nx = nxh * nxl
    pieces, (dqn, dqr, dlat, drope, dwk, dwv, total) = refs[:-7], refs[-7:]
    y, x, z, core = places(grid, dp_ref[0], ctx_ref[0])
    dr = drope.shape[0]
    lat = dlat.shape[1]
    ch = key_ref.shape[0] // 2
    own_half = pl.ds(pl.multiple_of(core * ch, ch), ch)
    other_half = pl.ds(pl.multiple_of((1 - core) * ch, ch), ch)
    total[...] = key_ref[...].astype(F32)
    total[own_half, :] += mine[:ch].astype(F32)
    total[other_half, :] += other[:ch].astype(F32)
    if other.shape[0] > ch:
        total[other_half, :] += mine[ch : 2 * ch].astype(F32)
        total[own_half, :] += other[ch:].astype(F32)
    key = total[...]
    dlat[...] = key[:, :lat].astype(BF)
    drope[...] = key[:, lat:].T[:dr].astype(BF)
    q = add(q_ref[0], back_ref[...])
    dqn[...] = q[:, : dqn.shape[1]]
    dqr[...] = q[:, dqn.shape[1] :]
    y, x, z, core = places(grid, dp_ref[0], ctx_ref[0])
    hd = dwk.shape[1]
    dc = dwk.shape[2]
    per_core = heads // nc
    per_y = per_core // ny
    group = hd // nx
    for i, j, n, k in itertools.product(range(nc), range(ny), range(nx), range(per_y)):
        ref = pieces[i * ny + j]
        h = (core + i) % nc * per_core + (y - j + ny) % ny * per_y + k
        at = pl.multiple_of((x - n + nx) % nx * group, group)
        r = (n * 2 * per_y + k) * group
        dwk[h, pl.ds(at, group), :] = ref[r : r + group, :].astype(F32) * scale
        r += per_y * group
        for m in range(dc // hd):
            dwv[h, pl.ds(m * hd + at, group), :] = (
                ref[r : r + group, m * hd : (m + 1) * hd].astype(F32) * scale
            )


def final_call(grid, heads, hd, dr, scale, dp, ctx, key, mine, other, q, back, pieces):
    tokens = key.shape[0]
    dc = pieces[0].shape[1]
    return pl.pallas_call(
        functools.partial(final_kernel, grid, heads, scale),
        in_specs=[SMEM, SMEM] + [VMEM] * (5 + len(pieces)),
        out_specs=(VMEM,) * 6,
        out_shape=(
            jax.ShapeDtypeStruct((tokens, heads * hd), BF),
            jax.ShapeDtypeStruct((tokens, heads * dr), BF),
            jax.ShapeDtypeStruct((tokens, dc), BF),
            jax.ShapeDtypeStruct((dr, tokens), BF),
            jax.ShapeDtypeStruct((heads, hd, dc), F32),
            jax.ShapeDtypeStruct((heads, dc, hd), F32),
        ),
        scratch_shapes=[pltpu.VMEM(key.shape, F32)],
        compiler_params=vmem(16),
        name="outputs",
    )(dp, ctx, key, mine, other, q, back, *pieces)


def make_local(grid):
    ny, nxh, nz, nxl, nc = grid
    nx = nxh * nxl

    def all_perm(x, fn):
        pairs = []
        for y, xh, z, xl, c in itertools.product(*map(range, grid)):
            y2, xh2, z2, xl2, c2 = fn(y, xh, z, xl, c)
            src = (((y * nxh + xh) * nz + z) * nxl + xl) * nc + c
            dst = (((y2 * nxh + xh2) * nz + z2) * nxl + xl2) * nc + c2
            pairs.append((src, dst))
        return lax.ppermute(x, ("dp", "ctx"), pairs)

    def z_send(x, s):
        return all_perm(x, lambda y, xh, z, xl, c: (y, xh, (z + s) % nz, xl, c))

    def z_relay(x):
        return all_perm(x, lambda y, xh, z, xl, c: (y, xh, (z + 1 - 2 * c) % nz, xl, c))

    def z_flip(x, bit):
        return all_perm(x, lambda y, xh, z, xl, c: (y, xh, z ^ bit, xl, c))

    def xl_swap(x):
        return all_perm(x, lambda y, xh, z, xl, c: (y, xh, z, nxl - 1 - xl, c))

    def c_swap(x):
        return all_perm(x, lambda y, xh, z, xl, c: (y, xh, z, xl, nc - 1 - c))

    def y_send(x, s):
        return all_perm(x, lambda y, xh, z, xl, c: ((y + s) % ny, xh, z, xl, c))

    def x_send(x, s):
        def fn(y, xh, z, xl, c):
            x2 = (xh * nxl + xl + s) % nx
            return y, x2 // nxl, z, x2 % nxl, c

        return all_perm(x, fn)

    def by_x(x, hd):
        x = x.reshape(ny, x.shape[0] // ny, nx, hd // nx, x.shape[2])
        return x.transpose(0, 2, 1, 3, 4).reshape(ny, nx, -1, x.shape[4])

    def local(span_ids, q_nope, q_rope, w_uk, latent, rope_key, w_uv, d_out, lse, saved_out):
        dp = lax.axis_index("dp").astype(jnp.int32).reshape(1)
        ctx = lax.axis_index("ctx").astype(jnp.int32).reshape(1)
        heads, hd, dc = w_uk.shape
        dr = rope_key.shape[2]
        tokens = q_nope.shape[1]
        ch = tokens // 2
        seq_rows = tokens * nz * nxl * nc
        scaling = (hd + dr) ** (-0.5)
        grad_scale = (ny * nxh * seq_rows) ** (-0.5)

        key = key_call(latent[0], rope_key[0].T)
        pack, *dwv = own_call(
            grid, dp, ctx, q_nope[0], q_rope[0], d_out[0], saved_out[0], lse[0].T, w_uv
        )

        half = nz // 2
        back, ahead = key, key
        keys = [key]
        for s in range(1, half):
            back, ahead = z_send(back, 1), z_send(ahead, -1)
            if s == 1:
                back, ahead, pack = lax.optimization_barrier((back, ahead, pack))
            else:
                back, ahead = lax.optimization_barrier((back, ahead))
            keys += [back, ahead]
        middle = back
        keys += [z_send(back[:ch], 1), z_send(ahead[ch:], -1)]

        pack_x = xl_swap(pack)
        pack_c = c_swap(pack)
        pack_x, _ = lax.optimization_barrier((pack_x, middle))
        packs = [pack, pack_x, pack_c, c_swap(pack_x)]

        dwv, dwv_send = dwv
        dwv_got = c_swap(dwv_send)
        res = attn_call(grid, span_ids, dp, ctx, packs, keys, w_uk, w_uv, heads * dr, scaling)
        dk_own, dk_far, *dk, dk_send, dq, dq_send, dwk, dwk_send = res

        t = jnp.concatenate(
            [by_x(add(dwk, c_swap(dwk_send)), hd), by_x(add(dwv, dwv_got), hd)], axis=2
        )
        t = add(t[0], *[y_send(t[s], s) for s in range(1, ny)])
        t = add(t[0], *[x_send(t[s], s) for s in range(1, nx)])
        bit = 1
        while bit < nz:
            t = add(t, z_flip(t, bit))
            bit *= 2
        t = jnp.concatenate([t] + [x_send(t, s) for s in range(1, nx)], axis=0)
        pieces = [t] + [y_send(t, s) for s in range(1, ny)]
        pieces += [c_swap(p) for p in pieces]

        dk_got = c_swap(dk_send)
        relay = z_relay(jnp.concatenate([dk_far, dk_got[:ch]], axis=0))
        at = ch
        for i, mine in enumerate(dk):
            other = dk_got[at : at + tokens]
            if i == 0:
                parts = [add(mine[:ch], relay[:ch]), mine[ch:], add(other[:ch], relay[ch:]), other[ch:]]
            else:
                parts = [add(mine, relay[:tokens]), add(other, relay[tokens:])]
            relay = z_relay(jnp.concatenate(parts, axis=0))
            at += tokens
        dk_other = c_swap(relay[relay.shape[0] // 2 :])

        q = add(dq, c_swap(dq_send))
        back = xl_swap(q[1])

        d_q_nope, d_q_rope, d_latent, d_rope_key, d_w_uk, d_w_uv = final_call(
            grid, heads, hd, dr, grad_scale, dp, ctx, dk_own, relay, dk_other, q, back, pieces
        )
        return (d_q_nope[None], d_q_rope[None], d_latent[None], d_rope_key.T[None], d_w_uk, d_w_uv)

    return local


def solution(mesh):
    dp, ctx = mesh.shape["dp"], mesh.shape["ctx"]
    grid = (dp // 2, 2, ctx // 4, 2, 2)
    rows = P("dp", "ctx", None)
    in_specs = (P("dp", None), rows, rows, P(), rows, rows, P(), rows, rows, rows)
    out_specs = (rows, rows, rows, rows, P(), P())
    return jax.shard_map(
        make_local(grid), mesh=mesh, in_specs=in_specs, out_specs=out_specs, check_vma=False
    )
```
